32 devices in a mesh: feat: 4 (over y, x), ex: 8 (over z, core).
Axes of the slice: x: 2, y: 2, z: 4, core: 2. Of those that a mesh axis runs over, the one named last changes fastest.
Arguments:
- train_grads: bfloat16 [1024, 262144], P('ex', 'feat')
- target_grads: bfloat16 [256, 262144], P('ex', 'feat')
- signs: int32 [32, 8192], replicated, may hold values from -1 to 1, as said below
- block_order: int32 [32], replicated, may hold values from 0 to 31, each once
Outputs:
- train_features: bfloat16 [1024, 8192], P('ex', 'feat')
- cosines: float32 [1024, 8, 32], P('ex', None, 'feat')
The draws below stay inside these ranges and needn't reach their ends.
Inputs may be any that keep to these rules, and one draw needn't show every extreme that they name: `signs`: every entry is +1 or -1.
All inputs are finite; a program needn't handle non-finite values.
Results may differ from the reference program's by a relative error of at most 0.013.
Values may be sent and summed in bfloat16 or wider, within the bound.
No kernel may reach another device: no remote copies, remote signals or barrier semaphores. Data moves between devices by JAX's collectives and lax.ppermute only.
A program may use at most 64 MiB of HBM per device.

```python
import math
import jax
import jax.numpy as jnp
from jax import lax

P_SIZE = 8192
TGT_DEV = 32
F = 262144
NBLK = 32
EXAMPLES = 1024
TARGETS = 256
N_EX = 8


def shared_directions(key):
    return jax.random.normal(jax.random.fold_in(key, 11), (4, F), jnp.float32)


def draw_train_grads(key, part):
    directions = shared_directions(key)
    key = jax.random.fold_in(key, 1)
    pick_key, noise_key = jax.random.split(key, 2)
    picks = jax.random.randint(pick_key, (EXAMPLES,), 0, 4)
    noise = jax.random.normal(noise_key, (EXAMPLES, F), jnp.float32)
    return (noise + 0.8 * directions[picks]).astype(jnp.bfloat16)


def draw_target_grads(key, part):
    directions = shared_directions(key)
    key = jax.random.fold_in(key, 2)
    pick_key, noise_key = jax.random.split(key, 2)
    picks = jax.random.randint(pick_key, (TARGETS,), 0, 4)
    noise = jax.random.normal(noise_key, (TARGETS, F), jnp.float32)
    return (noise + 0.8 * directions[picks]).astype(jnp.bfloat16)


def draw_signs(key, part):
    key = jax.random.fold_in(key, 3)
    return 2 * jax.random.randint(key, (NBLK, P_SIZE), 0, 2) - 1


def setup_inputs(seed: int = 0) -> dict:
    seeds = jax.random.split(jax.random.key(seed), 5)
    return {
        "train_grads": draw_train_grads(jax.random.fold_in(seeds[4], 71), 0),
        "target_grads": draw_target_grads(jax.random.fold_in(seeds[4], 71), 0),
        "signs": draw_signs(jax.random.fold_in(seeds[4], 71), 0),
        "block_order": jax.random.permutation(seeds[3], NBLK).astype(jnp.int32),
    }


def hadamard(values):
    length_now = values.shape[-1]
    leading = values.shape[:-1]
    half_span = 1
    while half_span < length_now:
        grouped = values.reshape(leading + (length_now // (2 * half_span), 2, half_span))
        first_half = grouped[..., 0, :]
        second_half = grouped[..., 1, :]
        values = jnp.stack([first_half + second_half, first_half - second_half], axis=-2).reshape(leading + (length_now,))
        half_span = half_span * 2
    return values

def normalize(projected):
    widened = projected.astype(jnp.float32)
    row_scale = lax.rsqrt(lax.optimization_barrier(jnp.mean(widened * widened, axis=-1, keepdims=True)) + 1e-06)
    return (widened * row_scale).astype(jnp.bfloat16)

def project(gradients, signs, block_order):
    proj_width = signs.shape[1]
    row_count = gradients.shape[0]

    def add_block(running, inputs):
        position, sign_row = inputs
        block = lax.dynamic_slice_in_dim(gradients, (position * proj_width).astype(jnp.int32), proj_width, 1)
        return (running + block.astype(jnp.float32) * sign_row.astype(jnp.float32)[None, :], None)
    summed, unused = lax.scan(add_block, jnp.zeros((row_count, proj_width), jnp.float32), (block_order, signs))
    transformed = hadamard(summed) * (1.0 / math.sqrt(F))
    return normalize(transformed.astype(jnp.bfloat16))

def reference(train_grads, target_grads, signs, block_order):
    train_features = project(train_grads, signs, block_order)
    target_normed = project(target_grads, signs, block_order)
    products = jnp.dot(train_features, target_normed.T, preferred_element_type=jnp.float32) / P_SIZE
    cosines = products.reshape(EXAMPLES, N_EX, TGT_DEV)
    return (train_features, cosines)
```

```python
import functools
import math

import jax
import jax.numpy as jnp
import numpy as np
from jax import lax
from jax.experimental import pallas as pl
from jax.experimental.pallas import tpu as pltpu
from jax.sharding import PartitionSpec as P

ROWS = 16
LANES = 256
CHUNKS = (48, 80)
EPS = 1e-06
MIB = 1 << 20
HBM = pl.BlockSpec(memory_space=pltpu.HBM)
SMEM = pl.BlockSpec(memory_space=pltpu.SMEM)
VMEM = pl.BlockSpec(memory_space=pltpu.VMEM)
ANY = pl.BlockSpec(memory_space=pl.ANY)


def sign_matrix(order):
    matrix = np.ones((1, 1), np.float32)
    while matrix.shape[0] < order:
        matrix = np.block([[matrix, matrix], [matrix, -matrix]])
    return matrix


def butterfly(parts):
    parts, half = list(parts), 1
    while half < len(parts):
        for i in range(len(parts)):
            if not i & half:
                a, b = parts[i], parts[i | half]
                parts[i], parts[i | half] = a + b, a - b
        half *= 2
    return parts


def wide(value):
    return value.astype(jnp.float32)


def narrow(value):
    return value.astype(jnp.bfloat16)


def diagonal(size):
    return lax.broadcasted_iota(jnp.int32, (size, size), 0) == lax.broadcasted_iota(jnp.int32, (size, size), 1)


def as_row(column):
    return jnp.sum(jnp.where(diagonal(column.shape[0]), column, 0.0), axis=0, keepdims=True)


def as_column(row):
    return jnp.sum(jnp.where(diagonal(row.shape[1]), row, 0.0), axis=1, keepdims=True)


def call(kernel, out_shape, operands, specs, name, limit=16, scratch=(), after=None, flops=10**10):
    body = kernel
    if after is not None:
        place = len(operands)
        operands, specs = [*operands, after], [*specs, ANY]

        def body(*refs):
            kernel(*refs[:place], *refs[place + 1 :])

    return pl.pallas_call(
        body,
        out_shape=out_shape,
        in_specs=specs,
        out_specs=jax.tree.map(lambda unused: VMEM, out_shape),
        scratch_shapes=scratch,
        compiler_params=pltpu.CompilerParams(vmem_limit_bytes=limit * MIB),
        cost_estimate=pl.CostEstimate(flops=flops, bytes_accessed=0, transcendentals=0),
        name=name,
    )(*operands)


def fetch(first, gradients_ref, held, sems):
    tiles, blocks = sems.shape
    width = held.shape[2] // blocks
    copies = []
    for i in range(tiles):
        row = []
        for p in range(blocks):
            span = pl.ds(p * width, width)
            copy = pltpu.make_async_copy(
                gradients_ref.at[pl.ds(first + i * ROWS, ROWS), span], held.at[i, :, span], sems.at[i, p]
            )
            copy.start()
            row.append(copy)
        copies.append(row)
    return copies


def reverse_bits(number, count):
    return sum((number >> i & 1) << (count - 1 - i) for i in range(count))


def outer_terms(feat_count, core, spread, tiles, store, make_sign=None):
    blocks, unused, width = spread.shape
    inner = width // feat_count
    lanes = min(LANES, inner)
    count = feat_count.bit_length() - 1
    places = [
        pl.multiple_of(jnp.where(core == 0, h, reverse_bits(h, count)) * inner, inner) for h in range(feat_count)
    ]

    @pl.loop(0, inner // lanes)
    def step(c):
        start = pl.multiple_of(c * lanes, lanes)
        for i, tile in enumerate(tiles):
            sums = []
            for h in range(feat_count):
                span = pl.ds(pl.multiple_of(places[h] + start, lanes), lanes)
                if make_sign is not None and i == 0:
                    for p in range(blocks):
                        spread[p, :, span] = make_sign(p, span)
                total = None
                for p in range(blocks):
                    piece = tile[:, pl.ds(pl.multiple_of(p * width + places[h] + start, lanes), lanes)]
                    term = wide(piece * spread[p, :, span])
                    total = term if total is None else total + term
                sums.append(total)
            for d, value in enumerate(butterfly(sums)):
                store(d, pl.ds(i * ROWS, ROWS), pl.ds(start, lanes), narrow(value))


def first_kernel(feat_count, feat_ref, core_ref, order_hbm, signs_hbm, gradients_ref, *refs):
    outs, (spread, held, sems, order, signs, mine, place, few) = refs[:feat_count], refs[feat_count:]
    order_copy = pltpu.make_async_copy(order_hbm, order, few.at[0])
    order_copy.start()
    copies = fetch(0, gradients_ref, held, sems)
    feat = feat_ref[0]
    blocks, unused, width = spread.shape
    inner = width // feat_count
    order_copy.wait()
    for b in range(order.shape[0]):
        place[order[b]] = b
    sign_copies = []
    for p in range(blocks):
        row = place[feat * blocks + p]
        sign_copies.append(pltpu.make_async_copy(signs_hbm.at[pl.ds(row, 1)], signs.at[pl.ds(p, 1)], few.at[1 + p]))
        sign_copies[-1].start()
    for copy in sign_copies:
        copy.wait()
    for h in range(feat_count):
        bits = feat & h
        odd = 0
        for shift in range(feat_count.bit_length() - 1):
            odd = odd ^ ((bits >> shift) & 1)
        span = pl.ds(h * inner, inner)
        mine[:, span] = wide(signs[:, span] * (1 - 2 * odd))

    def make_sign(p, span):
        return narrow(jnp.broadcast_to(mine[pl.ds(p, 1), span], (ROWS, span.size)))

    def store(d, rows, lanes, value):
        outs[d][rows, lanes] = value

    for tile in copies:
        for copy in tile:
            copy.wait()
    tiles = [held.at[i] for i in range(held.shape[0])]
    outer_terms(feat_count, core_ref[0], spread, tiles, store, make_sign)


def first_terms(feat_count, feat, core, block_order, signs, gradients):
    rows, columns = gradients.shape
    total, width = signs.shape
    blocks = columns // width
    part = jax.ShapeDtypeStruct((rows, width // feat_count), jnp.bfloat16)
    *parts, table = call(
        functools.partial(first_kernel, feat_count),
        [part] * feat_count + [jax.ShapeDtypeStruct((blocks, ROWS, width), jnp.bfloat16)],
        [feat, core, block_order, signs, gradients],
        [SMEM, SMEM, HBM, HBM, HBM],
        "first_terms",
        flops=2 * 10**10,
        limit=7,
        scratch=[
            pltpu.VMEM((rows // ROWS, ROWS, columns), jnp.bfloat16),
            pltpu.SemaphoreType.DMA((rows // ROWS, blocks)),
            pltpu.SMEM((total,), jnp.int32),
            pltpu.VMEM((blocks, width), jnp.int32),
            pltpu.VMEM((blocks, width), jnp.float32),
            pltpu.SMEM((total,), jnp.int32),
            pltpu.SemaphoreType.DMA((1 + blocks,)),
        ],
    )
    return parts, table


def halving_places(bits):
    count = len(bits)
    numbers = [sum((d >> bit & 1) << (count - 1 - i) for i, bit in enumerate(bits)) for d in range(1 << count)]
    return [divmod(number, 1 << (count - 1)) for number in numbers]


def terms_kernel(first, places, core_ref, spread, gradients_ref, *outs):
    def store(d, rows, lanes, value):
        half, place = places[d]
        outs[half][place, rows, lanes] = value

    tiles = [gradients_ref.at[pl.ds(first + i, ROWS)] for i in range(0, outs[0].shape[1], ROWS)]
    outer_terms(len(places), core_ref[0], spread, tiles, store)


def terms(bits, core, table, gradients, first, rows, after):
    blocks, unused, width = table.shape
    feat_count = 1 << len(bits)
    columns = gradients.shape[1]
    part = jax.ShapeDtypeStruct((feat_count // 2, rows, width // feat_count), jnp.bfloat16)
    return call(
        functools.partial(terms_kernel, first, halving_places(bits)),
        [part, part],
        [core, table, gradients],
        [SMEM, VMEM, VMEM],
        "terms",
        limit=4,
        after=after,
    )


def add_parts(refs, low, high):
    total = wide(refs[0][low:high])
    for ref in refs[1:]:
        total = total + wide(ref[low:high])
    return total


def middle_kernel(low, high, *refs):
    refs[-1][...] = add_parts(refs[:-1], low, high).astype(refs[-1].dtype)


def middle(parts, low, high, after):
    return call(
        functools.partial(middle_kernel, low, high),
        jax.ShapeDtypeStruct((high - low, *parts[0].shape[1:]), parts[0].dtype),
        parts,
        [VMEM] * len(parts),
        "middle",
        limit=16,
        after=after,
    )


def combine_kernel(*refs):
    refs[-1][...] = narrow(add_parts(refs[:-1], 0, refs[-1].shape[0]))


def combine(parts, after):
    return call(
        combine_kernel,
        jax.ShapeDtypeStruct(parts[0].shape, jnp.bfloat16),
        parts,
        [VMEM] * len(parts),
        "combine",
        limit=16,
        after=after,
    )


def inner_part(scale, table, t1):
    side = table.shape[0]
    parts = butterfly(
        [
            jnp.dot(t1[:, c : c + side], table, preferred_element_type=jnp.float32)
            for c in range(0, t1.shape[1], side)
        ]
    )
    return narrow(jnp.concatenate(parts, axis=1) * scale)


def inner_table(width):
    return jnp.asarray(sign_matrix(min(256, width)), jnp.bfloat16)


def stack_kernel(feat_count, per, feat_ref, *refs):
    parts, out_ref = refs[:-1], refs[-1]
    feat = feat_ref[0]
    rows, inner = parts[0].shape
    count = rows * len(parts)
    columns = []
    for i, part in enumerate(parts):
        value = part[...]
        out_ref[pl.ds(i * rows, rows), :] = value
        columns.append(square_sums(value))
    place = lax.broadcasted_iota(jnp.int32, (count, count), 1)
    source = lax.broadcasted_iota(jnp.int32, (count, count), 0)
    share = count // feat_count
    d, left = place // share, place % share
    wanted = (left // per) * rows + (d ^ feat) * per + left % per
    norms = jnp.sum(jnp.where(source == wanted, jnp.concatenate(columns, axis=0), 0.0), axis=0, keepdims=True)
    pieces = []
    for unused in range(3):
        piece = narrow(norms)
        norms = norms - wide(piece)
        pieces.append(wide(piece))
    pieces = jnp.concatenate([*pieces, jnp.zeros((ROWS - 3, count), jnp.float32)], axis=0)
    out_ref[pl.ds(count, ROWS), pl.ds(0, count)] = narrow(pieces)
    if inner > count:
        out_ref[pl.ds(count, ROWS), pl.ds(count, inner - count)] = jnp.zeros((ROWS, inner - count), jnp.bfloat16)


def stack_targets(feat_count, per, feat, parts, after):
    rows, inner = parts[0].shape
    return call(
        functools.partial(stack_kernel, feat_count, per),
        jax.ShapeDtypeStruct((rows * len(parts) + ROWS, inner), jnp.bfloat16),
        [feat, *parts],
        [SMEM] + [VMEM] * len(parts),
        "stack_targets",
        after=after,
    )


def square_sums(value):
    value = wide(value)
    return jnp.sum(value * value, axis=1, keepdims=True)


def join_kernel(counts, *refs):
    parts, (t1_ref, norms_ref) = refs[: sum(counts)], refs[sum(counts) :]
    row, norms = 0, []
    for count in counts:
        chunk, parts = parts[:count], parts[count:]
        total = narrow(add_parts(chunk, 0, 1)[0])
        t1_ref[pl.ds(row, total.shape[0]), :] = total
        row += total.shape[0]
        norms.append(square_sums(total))
    norms = as_row(jnp.concatenate(norms, axis=0))
    norms_ref[...] = jnp.concatenate([norms, jnp.zeros((7, row), jnp.float32)], axis=0)


def join(chunks):
    parts = [part for chunk in chunks for part in chunk]
    rows = sum(chunk[0].shape[1] for chunk in chunks)
    return call(
        functools.partial(join_kernel, [len(chunk) for chunk in chunks]),
        [
            jax.ShapeDtypeStruct((rows, parts[0].shape[2]), jnp.bfloat16),
            jax.ShapeDtypeStruct((8, rows), jnp.float32),
        ],
        parts,
        [VMEM] * len(parts),
        "join",
    )


def gram_kernel(per, feat_ref, t1_ref, norms_ref, mine_ref, other_ref, *refs):
    outs, products = refs[:-1], refs[-1]
    feat = feat_ref[0]
    rows = t1_ref.shape[0]
    height = mine_ref.shape[0] - ROWS
    share = height // len(outs)
    target_norms = []
    for i, ref in enumerate((mine_ref, other_ref)):
        products[pl.ds(i * height, height), :] = lax.dot_general(
            ref[pl.ds(0, height), :], t1_ref[...], (((1,), (1,)), ((), ())), preferred_element_type=jnp.float32
        )
        pieces = wide(ref[pl.ds(height, ROWS), pl.ds(0, height)])
        target_norms.append(pieces[0:1] + pieces[1:2] + pieces[2:3])
    for d, out in enumerate(outs):
        for i in range(0, 2 * share, per):
            first = pl.multiple_of((i * len(outs)) + (d ^ feat) * per, per)
            out[pl.ds(i, per), :] = products[pl.ds(first, per), :]
        span = slice(d * share, (d + 1) * share)
        here = jnp.concatenate(
            [x[:, span] for x in target_norms] + [jnp.zeros((1, rows - 2 * share), jnp.float32)], axis=1
        )
        out[pl.ds(2 * share, 8), :] = jnp.concatenate([norms_ref[0:1, :], here, jnp.zeros((6, rows), jnp.float32)], axis=0)


def gram(feat_count, per, feat, t1, norms, mine, other):
    total = 2 * (mine.shape[0] - ROWS)
    rows = t1.shape[0]
    return call(
        functools.partial(gram_kernel, per),
        [jax.ShapeDtypeStruct((total // feat_count + 8, rows), jnp.float32)] * feat_count,
        [feat, t1, norms, mine, other],
        [SMEM] + [VMEM] * 4,
        "gram",
        scratch=[pltpu.VMEM((total, rows), jnp.float32)],
    )


def inner_kernel(scale, table_ref, t1_ref, out_ref):
    out_ref[...] = inner_part(scale, table_ref[...], t1_ref[...])


def inner_transform(scale, table, t1):
    return call(
        functools.partial(inner_kernel, scale),
        jax.ShapeDtypeStruct(t1.shape, jnp.bfloat16),
        [table, t1],
        [VMEM, VMEM],
        "inner_transform",
        limit=16,
    )


def finish_kernel(mean_scale, per, ex_ref, projected_ref, *refs):
    parts, (features_ref, cosines_ref) = refs[:-2], refs[-2:]
    count = cosines_ref.shape[0]
    share = count // 2
    sums = parts[0][...]
    for part in parts[1:]:
        sums = sums + part[...]
    train_scale = lax.rsqrt(sums[count : count + 1] * mean_scale + EPS)
    target_scale = lax.rsqrt(sums[count + 1 : count + 2, :count] * mean_scale + EPS)
    cosines = sums[:count] * train_scale * as_column(target_scale) * mean_scale
    for i in range(count // per):
        group = ex_ref[0] ^ (i * 2 if i * per < share else i * 2 - count // per + 1)
        cosines_ref[pl.ds(pl.multiple_of(group * per, per), per), :] = cosines[i * per : (i + 1) * per]
    features_ref[...] = narrow(wide(projected_ref[...]) * as_column(train_scale))


def finish(mean_scale, per, ex, projected, parts):
    return call(
        functools.partial(finish_kernel, mean_scale, per),
        [
            jax.ShapeDtypeStruct(projected.shape, jnp.bfloat16),
            jax.ShapeDtypeStruct((parts[0].shape[0] - 8, projected.shape[0]), jnp.float32),
        ],
        [ex, projected, *parts],
        [SMEM] + [VMEM] * (1 + len(parts)),
        "finish",
    )


def swap(value, axis, distance):
    return lax.ppermute(value, axis, [(i, i ^ distance) for i in range(lax.axis_size(axis))])


def local(train_grads, target_grads, signs, block_order):
    train_grads, target_grads, signs, block_order = (
        pltpu.with_memory_space_constraint(value, pltpu.HBM)
        for value in (train_grads, target_grads, signs, block_order)
    )
    train_grads = pltpu.with_memory_space_constraint(train_grads, pltpu.VMEM)
    block_total, width = signs.shape
    feat_count = lax.axis_size("feat")
    groups = lax.axis_size("ex")
    feat = lax.axis_index("feat").astype(jnp.int32).reshape(1)
    ex = lax.axis_index("ex").astype(jnp.int32)
    train_rows, target_rows = train_grads.shape[0], target_grads.shape[0]
    per = target_rows // feat_count
    inner = width // feat_count
    mean_scale = 1.0 / (block_total * width * feat_count)
    scale = 1.0 / math.sqrt(block_total * width)
    table256 = inner_table(inner)
    bits = list(range(feat_count.bit_length() - 1))
    assert sum(CHUNKS) == train_rows

    core = (ex % 2).reshape(1)

    def turn(value, d):
        other = reverse_bits(d, len(bits))
        pairs = [
            (f * groups + e, (f ^ (d if e % 2 == 0 else other)) * groups + e)
            for f in range(feat_count)
            for e in range(groups)
        ]
        return lax.ppermute(value, ("feat", "ex"), pairs)

    target_parts, table = first_terms(feat_count, feat, core, block_order, signs, target_grads)
    own = pltpu.with_memory_space_constraint(target_parts[0], pltpu.VMEM)
    got = [own] + [turn(target_parts[d], d) for d in range(1, feat_count)]

    orders = [bits if i % 2 == 0 else bits[::-1] for i in range(len(CHUNKS))]
    firsts = [sum(CHUNKS[:i]) for i in range(len(CHUNKS))]

    def start(i, after):
        keep, send = terms(orders[i], core, table, train_grads, firsts[i], CHUNKS[i], after)
        return [keep, turn(send, 1 << orders[i][0])], send

    def proceed(order, parts, after):
        for bit in order[1:]:
            high = parts[-1].shape[0]
            send = after = middle(parts, high // 2, high, after)
            parts = [*parts, turn(send, 1 << bit)]
        return parts, after

    state = [None] * len(CHUNKS)
    state[0], mark = start(0, None)
    state[1], mark = start(1, mark)
    own = combine(got, mark)
    around = [own] + [swap(own, "ex", d) for d in range(2, groups, 2)]
    state[0], mark = proceed(orders[0], state[0], own)
    state[1], mark = proceed(orders[1], state[1], mark)
    mine = stack_targets(feat_count, per, feat, around, mark)
    other = swap(mine, "ex", 1)
    t1, norms = join(state)
    sums = gram(feat_count, per, feat, t1, norms, mine, other)
    far = sorted(range(1, feat_count), key=lambda d: -d.bit_count())
    sums = [sums[0]] + [swap(sums[d], "feat", d) for d in far]
    projected = inner_transform(scale, table256, t1)
    features, cosines = finish(mean_scale, per, ex.reshape(1), projected, sums)
    return features, cosines.reshape(groups, per, train_rows).transpose(2, 0, 1)


def solution(mesh):
    placed = (P("ex", "feat"), P("ex", "feat"), P(), P())
    return jax.shard_map(
        local,
        mesh=mesh,
        in_specs=placed,
        out_specs=(P("ex", "feat"), P("ex", None, "feat")),
        check_vma=False,
    )
```

```python
import functools
import math

import jax
import jax.numpy as jnp
import numpy as np
from jax import lax
from jax.experimental import pallas as pl
from jax.experimental.pallas import tpu as pltpu
from jax.sharding import PartitionSpec as P

ROWS = 16
LANES = 256
CHUNKS = (48, 80)
EPS = 1e-06
MIB = 1 << 20
HBM = pl.BlockSpec(memory_space=pltpu.HBM)
SMEM = pl.BlockSpec(memory_space=pltpu.SMEM)
VMEM = pl.BlockSpec(memory_space=pltpu.VMEM)
ANY = pl.BlockSpec(memory_space=pl.ANY)


def sign_matrix(order):
    matrix = np.ones((1, 1), np.float32)
    while matrix.shape[0] < order:
        matrix = np.block([[matrix, matrix], [matrix, -matrix]])
    return matrix


def butterfly(parts):
    parts, half = list(parts), 1
    while half < len(parts):
        for i in range(len(parts)):
            if not i & half:
                a, b = parts[i], parts[i | half]
                parts[i], parts[i | half] = a + b, a - b
        half *= 2
    return parts


def wide(value):
    return value.astype(jnp.float32)


def narrow(value):
    return value.astype(jnp.bfloat16)


def diagonal(size):
    return lax.broadcasted_iota(jnp.int32, (size, size), 0) == lax.broadcasted_iota(jnp.int32, (size, size), 1)


def as_row(column):
    return jnp.sum(jnp.where(diagonal(column.shape[0]), column, 0.0), axis=0, keepdims=True)


def as_column(row):
    return jnp.sum(jnp.where(diagonal(row.shape[1]), row, 0.0), axis=1, keepdims=True)


def call(kernel, out_shape, operands, specs, name, limit=16, scratch=(), after=None, flops=10**10):
    body = kernel
    if after is not None:
        place = len(operands)
        operands, specs = [*operands, after], [*specs, ANY]

        def body(*refs):
            kernel(*refs[:place], *refs[place + 1 :])

    return pl.pallas_call(
        body,
        out_shape=out_shape,
        in_specs=specs,
        out_specs=jax.tree.map(lambda unused: VMEM, out_shape),
        scratch_shapes=scratch,
        compiler_params=pltpu.CompilerParams(vmem_limit_bytes=limit * MIB),
        cost_estimate=pl.CostEstimate(flops=flops, bytes_accessed=0, transcendentals=0),
        name=name,
    )(*operands)


def fetch(first, gradients_ref, held, sems):
    tiles, blocks = sems.shape
    width = held.shape[2] // blocks
    copies = []
    for i in range(tiles):
        row = []
        for p in range(blocks):
            span = pl.ds(p * width, width)
            copy = pltpu.make_async_copy(
                gradients_ref.at[pl.ds(first + i * ROWS, ROWS), span], held.at[i, :, span], sems.at[i, p]
            )
            copy.start()
            row.append(copy)
        copies.append(row)
    return copies


def reverse_bits(number, count):
    return sum((number >> i & 1) << (count - 1 - i) for i in range(count))


def outer_terms(feat_count, core, spread, tiles, store, make_sign=None):
    blocks, unused, width = spread.shape
    inner = width // feat_count
    lanes = min(LANES, inner)
    count = feat_count.bit_length() - 1
    places = [
        pl.multiple_of(jnp.where(core == 0, h, reverse_bits(h, count)) * inner, inner) for h in range(feat_count)
    ]

    @pl.loop(0, inner // lanes)
    def step(c):
        start = pl.multiple_of(c * lanes, lanes)
        for i, tile in enumerate(tiles):
            sums = []
            for h in range(feat_count):
                span = pl.ds(pl.multiple_of(places[h] + start, lanes), lanes)
                if make_sign is not None and i == 0:
                    for p in range(blocks):
                        spread[p, :, span] = make_sign(p, span)
                total = None
                for p in range(blocks):
                    piece = tile[:, pl.ds(pl.multiple_of(p * width + places[h] + start, lanes), lanes)]
                    term = wide(piece * spread[p, :, span])
                    total = term if total is None else total + term
                sums.append(total)
            for d, value in enumerate(butterfly(sums)):
                store(d, pl.ds(i * ROWS, ROWS), pl.ds(start, lanes), narrow(value))


def first_kernel(places, feat_ref, core_ref, order_hbm, signs_hbm, gradients_ref, *refs):
    outs, (spread, held, sems, order, signs, mine, place, few) = refs[:2], refs[2:]
    feat_count = len(places)
    order_copy = pltpu.make_async_copy(order_hbm, order, few.at[0])
    order_copy.start()
    copies = fetch(0, gradients_ref, held, sems)
    feat = feat_ref[0]
    blocks, unused, width = spread.shape
    inner = width // feat_count
    order_copy.wait()
    for b in range(order.shape[0]):
        place[order[b]] = b
    sign_copies = []
    for p in range(blocks):
        row = place[feat * blocks + p]
        sign_copies.append(pltpu.make_async_copy(signs_hbm.at[pl.ds(row, 1)], signs.at[pl.ds(p, 1)], few.at[1 + p]))
        sign_copies[-1].start()
    for copy in sign_copies:
        copy.wait()
    for h in range(feat_count):
        bits = feat & h
        odd = 0
        for shift in range(feat_count.bit_length() - 1):
            odd = odd ^ ((bits >> shift) & 1)
        span = pl.ds(h * inner, inner)
        mine[:, span] = wide(signs[:, span] * (1 - 2 * odd))

    def make_sign(p, span):
        return narrow(jnp.broadcast_to(mine[pl.ds(p, 1), span], (ROWS, span.size)))

    def store(d, rows, lanes, value):
        half, number = places[d]
        outs[half][number, rows, lanes] = value

    for tile in copies:
        for copy in tile:
            copy.wait()
    tiles = [held.at[i] for i in range(held.shape[0])]
    outer_terms(feat_count, core_ref[0], spread, tiles, store, make_sign)


def first_terms(bits, feat, core, block_order, signs, gradients):
    feat_count = 1 << len(bits)
    rows, columns = gradients.shape
    total, width = signs.shape
    blocks = columns // width
    part = jax.ShapeDtypeStruct((feat_count // 2, rows, width // feat_count), jnp.bfloat16)
    return call(
        functools.partial(first_kernel, halving_places(bits)),
        [part, part] + [jax.ShapeDtypeStruct((blocks, ROWS, width), jnp.bfloat16)],
        [feat, core, block_order, signs, gradients],
        [SMEM, SMEM, HBM, HBM, HBM],
        "first_terms",
        flops=2 * 10**10,
        limit=7,
        scratch=[
            pltpu.VMEM((rows // ROWS, ROWS, columns), jnp.bfloat16),
            pltpu.SemaphoreType.DMA((rows // ROWS, blocks)),
            pltpu.SMEM((total,), jnp.int32),
            pltpu.VMEM((blocks, width), jnp.int32),
            pltpu.VMEM((blocks, width), jnp.float32),
            pltpu.SMEM((total,), jnp.int32),
            pltpu.SemaphoreType.DMA((1 + blocks,)),
        ],
    )


def halving_places(bits):
    count = len(bits)
    numbers = [sum((d >> bit & 1) << (count - 1 - i) for i, bit in enumerate(bits)) for d in range(1 << count)]
    return [divmod(number, 1 << (count - 1)) for number in numbers]


def terms_kernel(first, places, core_ref, spread, gradients_ref, *outs):
    def store(d, rows, lanes, value):
        half, place = places[d]
        outs[half][place, rows, lanes] = value

    tiles = [gradients_ref.at[pl.ds(first + i, ROWS)] for i in range(0, outs[0].shape[1], ROWS)]
    outer_terms(len(places), core_ref[0], spread, tiles, store)


def terms(bits, core, table, gradients, first, rows, after):
    blocks, unused, width = table.shape
    feat_count = 1 << len(bits)
    columns = gradients.shape[1]
    part = jax.ShapeDtypeStruct((feat_count // 2, rows, width // feat_count), jnp.bfloat16)
    return call(
        functools.partial(terms_kernel, first, halving_places(bits)),
        [part, part],
        [core, table, gradients],
        [SMEM, VMEM, VMEM],
        "terms",
        limit=4,
        after=after,
    )


def add_parts(refs, low, high):
    total = wide(refs[0][low:high])
    for ref in refs[1:]:
        total = total + wide(ref[low:high])
    return total


def middle_kernel(low, high, *refs):
    refs[-1][...] = add_parts(refs[:-1], low, high).astype(refs[-1].dtype)


def middle(parts, low, high, after):
    return call(
        functools.partial(middle_kernel, low, high),
        jax.ShapeDtypeStruct((high - low, *parts[0].shape[1:]), parts[0].dtype),
        parts,
        [VMEM] * len(parts),
        "middle",
        limit=16,
        after=after,
    )


def combine_kernel(*refs):
    refs[-1][...] = narrow(add_parts(refs[:-1], 0, 1)[0])


def combine(parts, after):
    return call(
        combine_kernel,
        jax.ShapeDtypeStruct(parts[0].shape[1:], jnp.bfloat16),
        parts,
        [VMEM] * len(parts),
        "combine",
        limit=16,
        after=after,
    )


def inner_part(scale, table, t1):
    side = table.shape[0]
    parts = butterfly(
        [
            jnp.dot(t1[:, c : c + side], table, preferred_element_type=jnp.float32)
            for c in range(0, t1.shape[1], side)
        ]
    )
    return narrow(jnp.concatenate(parts, axis=1) * scale)


def inner_table(width):
    return jnp.asarray(sign_matrix(min(256, width)), jnp.bfloat16)


def stack_kernel(feat_count, per, feat_ref, *refs):
    parts, out_ref = refs[:-1], refs[-1]
    feat = feat_ref[0]
    rows, inner = parts[0].shape
    count = rows * len(parts)
    columns = []
    for i, part in enumerate(parts):
        value = part[...]
        out_ref[pl.ds(i * rows, rows), :] = value
        columns.append(square_sums(value))
    place = lax.broadcasted_iota(jnp.int32, (count, count), 1)
    source = lax.broadcasted_iota(jnp.int32, (count, count), 0)
    share = count // feat_count
    d, left = place // share, place % share
    wanted = (left // per) * rows + (d ^ feat) * per + left % per
    norms = jnp.sum(jnp.where(source == wanted, jnp.concatenate(columns, axis=0), 0.0), axis=0, keepdims=True)
    pieces = jnp.concatenate([*pieces_of(norms), jnp.zeros((ROWS - 3, count), jnp.float32)], axis=0)
    out_ref[pl.ds(count, ROWS), pl.ds(0, count)] = narrow(pieces)
    if inner > count:
        out_ref[pl.ds(count, ROWS), pl.ds(count, inner - count)] = jnp.zeros((ROWS, inner - count), jnp.bfloat16)


def stack_targets(feat_count, per, feat, parts, after):
    rows, inner = parts[0].shape
    return call(
        functools.partial(stack_kernel, feat_count, per),
        jax.ShapeDtypeStruct((rows * len(parts) + ROWS, inner), jnp.bfloat16),
        [feat, *parts],
        [SMEM] + [VMEM] * len(parts),
        "stack_targets",
        after=after,
    )


def pieces_of(row):
    pieces = []
    for unused in range(3):
        piece = wide(narrow(row))
        row = row - piece
        pieces.append(piece)
    return pieces


def square_sums(value):
    value = wide(value)
    return jnp.sum(value * value, axis=1, keepdims=True)


def join_kernel(counts, *refs):
    parts, (t1_ref, norms_ref) = refs[: sum(counts)], refs[sum(counts) :]
    row, norms = 0, []
    for count in counts:
        chunk, parts = parts[:count], parts[count:]
        total = narrow(add_parts(chunk, 0, 1)[0])
        t1_ref[pl.ds(row, total.shape[0]), :] = total
        row += total.shape[0]
        norms.append(square_sums(total))
    norms = as_row(jnp.concatenate(norms, axis=0))
    norms_ref[...] = jnp.concatenate([norms, jnp.zeros((7, row), jnp.float32)], axis=0)


def join(chunks):
    parts = [part for chunk in chunks for part in chunk]
    rows = sum(chunk[0].shape[1] for chunk in chunks)
    return call(
        functools.partial(join_kernel, [len(chunk) for chunk in chunks]),
        [
            jax.ShapeDtypeStruct((rows, parts[0].shape[2]), jnp.bfloat16),
            jax.ShapeDtypeStruct((8, rows), jnp.float32),
        ],
        parts,
        [VMEM] * len(parts),
        "join",
    )


def gram_kernel(per, feat_ref, t1_ref, norms_ref, mine_ref, other_ref, *refs):
    outs, products = refs[:-1], refs[-1]
    feat = feat_ref[0]
    rows = t1_ref.shape[0]
    height = mine_ref.shape[0] - ROWS
    share = height // len(outs)
    target_norms = []
    for i, ref in enumerate((mine_ref, other_ref)):
        products[pl.ds(i * height, height), :] = lax.dot_general(
            ref[pl.ds(0, height), :], t1_ref[...], (((1,), (1,)), ((), ())), preferred_element_type=jnp.float32
        )
        pieces = wide(ref[pl.ds(height, ROWS), pl.ds(0, height)])
        target_norms.append(pieces[0:1] + pieces[1:2] + pieces[2:3])
    for d, out in enumerate(outs):
        blocks = []
        for i in range(0, 2 * share, per):
            first = pl.multiple_of((i * len(outs)) + (d ^ feat) * per, per)
            blocks.append(products[pl.ds(first, per), :])
        span = slice(d * share, (d + 1) * share)
        here = jnp.concatenate(
            [x[:, span] for x in target_norms] + [jnp.zeros((1, rows - 2 * share), jnp.float32)], axis=1
        )
        sums = [norms_ref[0:1, :], here]
        if d > 0:
            sums = [piece for row in sums for piece in pieces_of(row)]
        sums.append(jnp.zeros((out.shape[0] - 2 * share - len(sums), rows), jnp.float32))
        out[...] = jnp.concatenate([*blocks, *sums], axis=0).astype(out.dtype)


def gram(feat_count, per, feat, t1, norms, mine, other):
    total = 2 * (mine.shape[0] - ROWS)
    rows = t1.shape[0]
    return call(
        functools.partial(gram_kernel, per),
        [jax.ShapeDtypeStruct((total // feat_count + 8, rows), jnp.float32)]
        + [jax.ShapeDtypeStruct((total // feat_count + ROWS, rows), jnp.bfloat16)] * (feat_count - 1),
        [feat, t1, norms, mine, other],
        [SMEM] + [VMEM] * 4,
        "gram",
        scratch=[pltpu.VMEM((total, rows), jnp.float32)],
    )


def inner_kernel(scale, table_ref, t1_ref, out_ref):
    out_ref[...] = inner_part(scale, table_ref[...], t1_ref[...])


def inner_transform(scale, table, t1):
    return call(
        functools.partial(inner_kernel, scale),
        jax.ShapeDtypeStruct(t1.shape, jnp.bfloat16),
        [table, t1],
        [VMEM, VMEM],
        "inner_transform",
        limit=16,
    )


def finish_kernel(mean_scale, per, ex_ref, projected_ref, *refs):
    parts, (features_ref, cosines_ref) = refs[:-2], refs[-2:]
    count = cosines_ref.shape[0]
    share = count // 2
    sums = parts[0][...]
    products, train_sums, target_sums = sums[:count], sums[count : count + 1], sums[count + 1 : count + 2]
    for part in parts[1:]:
        got = wide(part[...])
        products = products + got[:count]
        for i in range(count, count + 3):
            train_sums = train_sums + got[i : i + 1]
            target_sums = target_sums + got[i + 3 : i + 4]
    train_scale = lax.rsqrt(train_sums * mean_scale + EPS)
    target_scale = lax.rsqrt(target_sums[:, :count] * mean_scale + EPS)
    cosines = products * train_scale * as_column(target_scale) * mean_scale
    for i in range(count // per):
        group = ex_ref[0] ^ (i * 2 if i * per < share else i * 2 - count // per + 1)
        cosines_ref[pl.ds(pl.multiple_of(group * per, per), per), :] = cosines[i * per : (i + 1) * per]
    features_ref[...] = narrow(wide(projected_ref[...]) * as_column(train_scale))


def finish(mean_scale, per, ex, projected, parts):
    return call(
        functools.partial(finish_kernel, mean_scale, per),
        [
            jax.ShapeDtypeStruct(projected.shape, jnp.bfloat16),
            jax.ShapeDtypeStruct((parts[0].shape[0] - 8, projected.shape[0]), jnp.float32),
        ],
        [ex, projected, *parts],
        [SMEM] + [VMEM] * (1 + len(parts)),
        "finish",
    )


def swap(value, axis, distance):
    return lax.ppermute(value, axis, [(i, i ^ distance) for i in range(lax.axis_size(axis))])


def local(train_grads, target_grads, signs, block_order):
    train_grads, target_grads, signs, block_order = (
        pltpu.with_memory_space_constraint(value, pltpu.HBM)
        for value in (train_grads, target_grads, signs, block_order)
    )
    train_grads = pltpu.with_memory_space_constraint(train_grads, pltpu.VMEM)
    block_total, width = signs.shape
    feat_count = lax.axis_size("feat")
    groups = lax.axis_size("ex")
    feat = lax.axis_index("feat").astype(jnp.int32).reshape(1)
    ex = lax.axis_index("ex").astype(jnp.int32)
    train_rows, target_rows = train_grads.shape[0], target_grads.shape[0]
    per = target_rows // feat_count
    inner = width // feat_count
    mean_scale = 1.0 / (block_total * width * feat_count)
    scale = 1.0 / math.sqrt(block_total * width)
    table256 = inner_table(inner)
    bits = list(range(feat_count.bit_length() - 1))
    assert sum(CHUNKS) == train_rows

    core = (ex % 2).reshape(1)

    def turn(value, d):
        other = reverse_bits(d, len(bits))
        pairs = [
            (f * groups + e, (f ^ (d if e % 2 == 0 else other)) * groups + e)
            for f in range(feat_count)
            for e in range(groups)
        ]
        return lax.ppermute(value, ("feat", "ex"), pairs)

    keep, send, table = first_terms(bits, feat, core, block_order, signs, target_grads)
    got = [pltpu.with_memory_space_constraint(keep, pltpu.VMEM), turn(send, 1 << bits[0])]

    orders = [bits if i % 2 == 0 else bits[::-1] for i in range(len(CHUNKS))]
    firsts = [sum(CHUNKS[:i]) for i in range(len(CHUNKS))]

    def start(i, after):
        keep, send = terms(orders[i], core, table, train_grads, firsts[i], CHUNKS[i], after)
        return [keep, turn(send, 1 << orders[i][0])], send

    def proceed(order, parts, after):
        for bit in order[1:]:
            high = parts[-1].shape[0]
            send = after = middle(parts, high // 2, high, after)
            parts = [*parts, turn(send, 1 << bit)]
        return parts, after

    state = [None] * len(CHUNKS)
    state[0], mark = start(0, None)
    got, mark = proceed(bits, got, mark)
    state[1], mark = start(1, mark)
    own = combine(got, mark)
    around = [own] + [swap(own, "ex", d) for d in range(2, groups, 2)]
    state[0], mark = proceed(orders[0], state[0], own)
    state[1], mark = proceed(orders[1], state[1], mark)
    mine = stack_targets(feat_count, per, feat, around, mark)
    other = swap(mine, "ex", 1)
    t1, norms = join(state)
    sums = gram(feat_count, per, feat, t1, norms, mine, other)
    far = sorted(range(1, feat_count), key=lambda d: -d.bit_count())
    sums = [sums[0]] + [swap(sums[d], "feat", d) for d in far]
    projected = inner_transform(scale, table256, t1)
    features, cosines = finish(mean_scale, per, ex.reshape(1), projected, sums)
    return features, cosines.reshape(groups, per, train_rows).transpose(2, 0, 1)


def solution(mesh):
    placed = (P("ex", "feat"), P("ex", "feat"), P(), P())
    return jax.shard_map(
        local,
        mesh=mesh,
        in_specs=placed,
        out_specs=(P("ex", "feat"), P("ex", None, "feat")),
        check_vma=False,
    )
```

```python
import functools
import math

import jax
import jax.numpy as jnp
import numpy as np
from jax import lax
from jax.experimental import pallas as pl
from jax.experimental.pallas import tpu as pltpu
from jax.sharding import PartitionSpec as P

ROWS = 16
LANES = 512
CHUNKS = (48, 80)
EPS = 1e-06
MIB = 1 << 20
HBM = pl.BlockSpec(memory_space=pltpu.HBM)
SMEM = pl.BlockSpec(memory_space=pltpu.SMEM)
VMEM = pl.BlockSpec(memory_space=pltpu.VMEM)
ANY = pl.BlockSpec(memory_space=pl.ANY)


def sign_matrix(order):
    matrix = np.ones((1, 1), np.float32)
    while matrix.shape[0] < order:
        matrix = np.block([[matrix, matrix], [matrix, -matrix]])
    return matrix


def butterfly(parts):
    parts, half = list(parts), 1
    while half < len(parts):
        for i in range(len(parts)):
            if not i & half:
                a, b = parts[i], parts[i | half]
                parts[i], parts[i | half] = a + b, a - b
        half *= 2
    return parts


def wide(value):
    return value.astype(jnp.float32)


def narrow(value):
    return value.astype(jnp.bfloat16)


def diagonal(size):
    return lax.broadcasted_iota(jnp.int32, (size, size), 0) == lax.broadcasted_iota(jnp.int32, (size, size), 1)


def as_row(column):
    return jnp.sum(jnp.where(diagonal(column.shape[0]), column, 0.0), axis=0, keepdims=True)


def as_column(row):
    return jnp.sum(jnp.where(diagonal(row.shape[1]), row, 0.0), axis=1, keepdims=True)


def call(kernel, out_shape, operands, specs, name, limit=16, scratch=(), after=None, flops=10**10):
    body = kernel
    if after is not None:
        place = len(operands)
        operands, specs = [*operands, after], [*specs, ANY]

        def body(*refs):
            kernel(*refs[:place], *refs[place + 1 :])

    return pl.pallas_call(
        body,
        out_shape=out_shape,
        in_specs=specs,
        out_specs=jax.tree.map(lambda unused: VMEM, out_shape),
        scratch_shapes=scratch,
        compiler_params=pltpu.CompilerParams(vmem_limit_bytes=limit * MIB),
        cost_estimate=pl.CostEstimate(flops=flops, bytes_accessed=0, transcendentals=0),
        name=name,
    )(*operands)


def fetch(first, gradients_ref, held, sems):
    tiles, blocks = sems.shape
    width = held.shape[2] // blocks
    copies = []
    for i in range(tiles):
        row = []
        for p in range(blocks):
            span = pl.ds(p * width, width)
            copy = pltpu.make_async_copy(
                gradients_ref.at[pl.ds(first + i * ROWS, ROWS), span], held.at[i, :, span], sems.at[i, p]
            )
            copy.start()
            row.append(copy)
        copies.append(row)
    return copies


def reverse_bits(number, count):
    return sum((number >> i & 1) << (count - 1 - i) for i in range(count))


def outer_terms(feat_count, core, spread, tiles, store, make_sign=None):
    blocks, unused, width = spread.shape
    inner = width // feat_count
    lanes = min(LANES, inner)
    count = feat_count.bit_length() - 1
    places = [
        pl.multiple_of(jnp.where(core == 0, h, reverse_bits(h, count)) * inner, inner) for h in range(feat_count)
    ]

    @pl.loop(0, inner // lanes)
    def step(c):
        start = pl.multiple_of(c * lanes, lanes)
        for i, tile in enumerate(tiles):
            sums = []
            for h in range(feat_count):
                span = pl.ds(pl.multiple_of(places[h] + start, lanes), lanes)
                if make_sign is not None and i == 0:
                    for p in range(blocks):
                        spread[p, :, span] = make_sign(p, span)
                total = None
                for p in range(0, blocks, 2):
                    pair = [
                        tile[:, pl.ds(pl.multiple_of(q * width + places[h] + start, lanes), lanes)] * spread[q, :, span]
                        for q in range(p, min(p + 2, blocks))
                    ]
                    term = wide(sum(pair[1:], pair[0]))
                    total = term if total is None else total + term
                sums.append(total)
            for d, value in enumerate(butterfly(sums)):
                store(d, pl.ds(i * ROWS, ROWS), pl.ds(start, lanes), narrow(value))


def first_kernel(feat_count, feat_ref, core_ref, order_hbm, signs_hbm, gradients_ref, *refs):
    outs, (spread, held, sems, order, signs, mine, place, few) = refs[:feat_count], refs[feat_count:]
    order_copy = pltpu.make_async_copy(order_hbm, order, few.at[0])
    order_copy.start()
    copies = fetch(0, gradients_ref, held, sems)
    feat = feat_ref[0]
    blocks, unused, width = spread.shape
    inner = width // feat_count
    order_copy.wait()
    for b in range(order.shape[0]):
        place[order[b]] = b
    sign_copies = []
    for p in range(blocks):
        row = place[feat * blocks + p]
        sign_copies.append(pltpu.make_async_copy(signs_hbm.at[pl.ds(row, 1)], signs.at[pl.ds(p, 1)], few.at[1 + p]))
        sign_copies[-1].start()
    for copy in sign_copies:
        copy.wait()
    for h in range(feat_count):
        bits = feat & h
        odd = 0
        for shift in range(feat_count.bit_length() - 1):
            odd = odd ^ ((bits >> shift) & 1)
        span = pl.ds(h * inner, inner)
        mine[:, span] = wide(signs[:, span] * (1 - 2 * odd))

    def make_sign(p, span):
        return narrow(jnp.broadcast_to(mine[pl.ds(p, 1), span], (ROWS, span.size)))

    def store(d, rows, lanes, value):
        outs[d][rows, lanes] = value

    for tile in copies:
        for copy in tile:
            copy.wait()
    tiles = [held.at[i] for i in range(held.shape[0])]
    outer_terms(feat_count, core_ref[0], spread, tiles, store, make_sign)


def first_terms(feat_count, feat, core, block_order, signs, gradients):
    rows, columns = gradients.shape
    total, width = signs.shape
    blocks = columns // width
    part = jax.ShapeDtypeStruct((rows, width // feat_count), jnp.bfloat16)
    *parts, table = call(
        functools.partial(first_kernel, feat_count),
        [part] * feat_count + [jax.ShapeDtypeStruct((blocks, ROWS, width), jnp.bfloat16)],
        [feat, core, block_order, signs, gradients],
        [SMEM, SMEM, HBM, HBM, HBM],
        "first_terms",
        flops=2 * 10**10,
        limit=7,
        scratch=[
            pltpu.VMEM((rows // ROWS, ROWS, columns), jnp.bfloat16),
            pltpu.SemaphoreType.DMA((rows // ROWS, blocks)),
            pltpu.SMEM((total,), jnp.int32),
            pltpu.VMEM((blocks, width), jnp.int32),
            pltpu.VMEM((blocks, width), jnp.float32),
            pltpu.SMEM((total,), jnp.int32),
            pltpu.SemaphoreType.DMA((1 + blocks,)),
        ],
    )
    return parts, table


def halving_places(bits):
    count = len(bits)
    numbers = [sum((d >> bit & 1) << (count - 1 - i) for i, bit in enumerate(bits)) for d in range(1 << count)]
    return [divmod(number, 1 << (count - 1)) for number in numbers]


def terms_kernel(first, places, core_ref, spread, gradients_ref, *outs):
    def store(d, rows, lanes, value):
        half, place = places[d]
        outs[half][place, rows, lanes] = value

    tiles = [gradients_ref.at[pl.ds(first + i, ROWS)] for i in range(0, outs[0].shape[1], ROWS)]
    outer_terms(len(places), core_ref[0], spread, tiles, store)


def terms(bits, core, table, gradients, first, rows, after):
    blocks, unused, width = table.shape
    feat_count = 1 << len(bits)
    columns = gradients.shape[1]
    part = jax.ShapeDtypeStruct((feat_count // 2, rows, width // feat_count), jnp.bfloat16)
    return call(
        functools.partial(terms_kernel, first, halving_places(bits)),
        [part, part],
        [core, table, gradients],
        [SMEM, VMEM, VMEM],
        "terms",
        limit=4,
        after=after,
    )


def add_parts(refs, low, high):
    total = wide(refs[0][low:high])
    for ref in refs[1:]:
        total = total + wide(ref[low:high])
    return total


def middle_kernel(low, high, *refs):
    refs[-1][...] = add_parts(refs[:-1], low, high).astype(refs[-1].dtype)


def middle(parts, low, high, after):
    return call(
        functools.partial(middle_kernel, low, high),
        jax.ShapeDtypeStruct((high - low, *parts[0].shape[1:]), parts[0].dtype),
        parts,
        [VMEM] * len(parts),
        "middle",
        limit=16,
        after=after,
    )


def combine_kernel(*refs):
    refs[-1][...] = narrow(add_parts(refs[:-1], 0, refs[-1].shape[0]))


def combine(parts, after):
    return call(
        combine_kernel,
        jax.ShapeDtypeStruct(parts[0].shape, jnp.bfloat16),
        parts,
        [VMEM] * len(parts),
        "combine",
        limit=16,
        after=after,
    )


def inner_part(scale, table, t1):
    side = table.shape[0]
    parts = butterfly(
        [
            jnp.dot(t1[:, c : c + side], table, preferred_element_type=jnp.float32)
            for c in range(0, t1.shape[1], side)
        ]
    )
    return narrow(jnp.concatenate(parts, axis=1) * scale)


def inner_table(width):
    return jnp.asarray(sign_matrix(min(256, width)), jnp.bfloat16)


def stack_kernel(feat_count, per, feat_ref, *refs):
    parts, out_ref = refs[:-1], refs[-1]
    feat = feat_ref[0]
    rows, inner = parts[0].shape
    count = rows * len(parts)
    columns = []
    for i, part in enumerate(parts):
        value = part[...]
        out_ref[pl.ds(i * rows, rows), :] = value
        columns.append(square_sums(value))
    place = lax.broadcasted_iota(jnp.int32, (count, count), 1)
    source = lax.broadcasted_iota(jnp.int32, (count, count), 0)
    share = count // feat_count
    d, left = place // share, place % share
    wanted = (left // per) * rows + (d ^ feat) * per + left % per
    norms = jnp.sum(jnp.where(source == wanted, jnp.concatenate(columns, axis=0), 0.0), axis=0, keepdims=True)
    pieces = []
    for unused in range(3):
        piece = narrow(norms)
        norms = norms - wide(piece)
        pieces.append(wide(piece))
    pieces = jnp.concatenate([*pieces, jnp.zeros((ROWS - 3, count), jnp.float32)], axis=0)
    out_ref[pl.ds(count, ROWS), pl.ds(0, count)] = narrow(pieces)
    if inner > count:
        out_ref[pl.ds(count, ROWS), pl.ds(count, inner - count)] = jnp.zeros((ROWS, inner - count), jnp.bfloat16)


def stack_targets(feat_count, per, feat, parts, after):
    rows, inner = parts[0].shape
    return call(
        functools.partial(stack_kernel, feat_count, per),
        jax.ShapeDtypeStruct((rows * len(parts) + ROWS, inner), jnp.bfloat16),
        [feat, *parts],
        [SMEM] + [VMEM] * len(parts),
        "stack_targets",
        after=after,
    )


def square_sums(value):
    value = wide(value)
    return jnp.sum(value * value, axis=1, keepdims=True)


def join_kernel(*refs):
    refs[-1][...] = narrow(add_parts(refs[:-1], 0, 1)[0])


def join(parts):
    return call(
        join_kernel,
        jax.ShapeDtypeStruct(parts[0].shape[1:], jnp.bfloat16),
        parts,
        [VMEM] * len(parts),
        "join",
    )


def gram_kernel(per, feat_ref, core_ref, mine_ref, other_ref, first_ref, *refs):
    parts, last_ref, outs, products = refs[0], refs[1], refs[2], refs[3]
    feat = feat_ref[0]
    last = narrow(add_parts(parts, 0, 1)[0])
    last_ref[...] = last
    train = jnp.concatenate([first_ref[...], last], axis=0)
    rows = train.shape[0]
    height = mine_ref.shape[0] - ROWS
    share = height // len(outs)
    target_norms = []
    for i, ref in enumerate((mine_ref, other_ref)):
        products[pl.ds(i * height, height), :] = lax.dot_general(
            ref[pl.ds(0, height), :], train, (((1,), (1,)), ((), ())), preferred_element_type=jnp.float32
        )
        pieces = wide(ref[pl.ds(height, ROWS), pl.ds(0, height)])
        target_norms.append(pieces[0:1] + pieces[1:2] + pieces[2:3])
    norms = as_row(square_sums(train))
    count = len(outs).bit_length() - 1
    for d, out in enumerate(outs):
        turned = reverse_bits(d, count)
        number = jnp.where(core_ref[0] == 0, d, turned)
        for i in range(0, 2 * share, per):
            first = pl.multiple_of((i * len(outs)) + (number ^ feat) * per, per)
            out[pl.ds(i, per), :] = products[pl.ds(first, per), :]
        straight, crossed = (
            jnp.concatenate([x[:, i * share : (i + 1) * share] for x in target_norms], axis=1) for i in (d, turned)
        )
        here = jnp.concatenate(
            [jnp.where(core_ref[0] == 0, straight, crossed), jnp.zeros((1, rows - 2 * share), jnp.float32)], axis=1
        )
        out[pl.ds(2 * share, 8), :] = jnp.concatenate([norms, here, jnp.zeros((6, rows), jnp.float32)], axis=0)


def gram(feat_count, per, feat, core, mine, other, first, parts):
    total = 2 * (mine.shape[0] - ROWS)
    unused, last_rows, inner = parts[0].shape
    rows = first.shape[0] + last_rows

    def kernel(*refs):
        split = 5 + len(parts)
        gram_kernel(per, *refs[:5], refs[5:split], refs[split], refs[split + 1 : -1], refs[-1])

    last, *outs = call(
        kernel,
        [jax.ShapeDtypeStruct((last_rows, inner), jnp.bfloat16)]
        + [jax.ShapeDtypeStruct((total // feat_count + 8, rows), jnp.float32)] * feat_count,
        [feat, core, mine, other, first, *parts],
        [SMEM, SMEM] + [VMEM] * (3 + len(parts)),
        "gram",
        scratch=[pltpu.VMEM((total, rows), jnp.float32)],
    )
    return last, outs


def inner_kernel(scale, table_ref, *refs):
    row = 0
    for ref in refs[:-1]:
        rows = ref.shape[0]
        refs[-1][pl.ds(row, rows), :] = inner_part(scale, table_ref[...], ref[...])
        row += rows


def inner_transform(scale, table, chunks):
    rows = sum(chunk.shape[0] for chunk in chunks)
    return call(
        functools.partial(inner_kernel, scale),
        jax.ShapeDtypeStruct((rows, chunks[0].shape[1]), jnp.bfloat16),
        [table, *chunks],
        [VMEM] * (1 + len(chunks)),
        "inner_transform",
        limit=16,
    )


def finish_kernel(mean_scale, per, ex_ref, projected_ref, *refs):
    parts, (features_ref, cosines_ref) = refs[:-2], refs[-2:]
    count = cosines_ref.shape[0]
    share = count // 2
    sums = parts[0][...]
    for part in parts[1:]:
        sums = sums + part[...]
    train_scale = lax.rsqrt(sums[count : count + 1] * mean_scale + EPS)
    target_scale = lax.rsqrt(sums[count + 1 : count + 2, :count] * mean_scale + EPS)
    cosines = sums[:count] * train_scale * as_column(target_scale) * mean_scale
    for i in range(count // per):
        group = ex_ref[0] ^ (i * 2 if i * per < share else i * 2 - count // per + 1)
        cosines_ref[pl.ds(pl.multiple_of(group * per, per), per), :] = cosines[i * per : (i + 1) * per]
    features_ref[...] = narrow(wide(projected_ref[...]) * as_column(train_scale))


def finish(mean_scale, per, ex, projected, parts):
    return call(
        functools.partial(finish_kernel, mean_scale, per),
        [
            jax.ShapeDtypeStruct(projected.shape, jnp.bfloat16),
            jax.ShapeDtypeStruct((parts[0].shape[0] - 8, projected.shape[0]), jnp.float32),
        ],
        [ex, projected, *parts],
        [SMEM] + [VMEM] * (1 + len(parts)),
        "finish",
    )


def swap(value, axis, distance):
    return lax.ppermute(value, axis, [(i, i ^ distance) for i in range(lax.axis_size(axis))])


def local(train_grads, target_grads, signs, block_order):
    train_grads, target_grads, signs, block_order = (
        pltpu.with_memory_space_constraint(value, pltpu.HBM)
        for value in (train_grads, target_grads, signs, block_order)
    )
    train_grads = pltpu.with_memory_space_constraint(train_grads, pltpu.VMEM)
    block_total, width = signs.shape
    feat_count = lax.axis_size("feat")
    groups = lax.axis_size("ex")
    feat = lax.axis_index("feat").astype(jnp.int32).reshape(1)
    ex = lax.axis_index("ex").astype(jnp.int32)
    train_rows, target_rows = train_grads.shape[0], target_grads.shape[0]
    per = target_rows // feat_count
    inner = width // feat_count
    mean_scale = 1.0 / (block_total * width * feat_count)
    scale = 1.0 / math.sqrt(block_total * width)
    table256 = inner_table(inner)
    bits = list(range(feat_count.bit_length() - 1))
    assert sum(CHUNKS) == train_rows

    core = (ex % 2).reshape(1)

    def turn(value, d):
        other = reverse_bits(d, len(bits))
        pairs = [
            (f * groups + e, (f ^ (d if e % 2 == 0 else other)) * groups + e)
            for f in range(feat_count)
            for e in range(groups)
        ]
        return lax.ppermute(value, ("feat", "ex"), pairs)

    target_parts, table = first_terms(feat_count, feat, core, block_order, signs, target_grads)
    own = pltpu.with_memory_space_constraint(target_parts[0], pltpu.VMEM)
    got = [own] + [turn(target_parts[d], d) for d in range(1, feat_count)]

    orders = [bits if i % 2 == 0 else bits[::-1] for i in range(len(CHUNKS))]
    firsts = [sum(CHUNKS[:i]) for i in range(len(CHUNKS))]

    def start(i, after):
        keep, send = terms(orders[i], core, table, train_grads, firsts[i], CHUNKS[i], after)
        return [keep, turn(send, 1 << orders[i][0])], send

    def proceed(order, parts, after):
        for bit in order[1:]:
            high = parts[-1].shape[0]
            send = after = middle(parts, high // 2, high, after)
            parts = [*parts, turn(send, 1 << bit)]
        return parts, after

    state = [None] * len(CHUNKS)
    state[0], mark = start(0, None)
    state[1], mark = start(1, mark)
    own = combine(got, mark)
    around = [own] + [swap(own, "ex", d) for d in range(2, groups, 2)]
    state[0], mark = proceed(orders[0], state[0], own)
    state[1], mark = proceed(orders[1], state[1], mark)
    mine = stack_targets(feat_count, per, feat, around, mark)
    other = swap(mine, "ex", 1)
    first = join(state[0])
    last, sums = gram(feat_count, per, feat, core, mine, other, first, state[1])
    far = sorted(range(1, feat_count), key=lambda d: -d.bit_count())
    sums = [sums[0]] + [turn(sums[d], d) for d in far]
    projected = inner_transform(scale, table256, [first, last])
    features, cosines = finish(mean_scale, per, ex.reshape(1), projected, sums)
    return features, cosines.reshape(groups, per, train_rows).transpose(2, 0, 1)


def solution(mesh):
    placed = (P("ex", "feat"), P("ex", "feat"), P(), P())
    return jax.shard_map(
        local,
        mesh=mesh,
        in_specs=placed,
        out_specs=(P("ex", "feat"), P("ex", None, "feat")),
        check_vma=False,
    )
```

```python
import functools
import math

import jax
import jax.numpy as jnp
import numpy as np
from jax import lax
from jax.experimental import pallas as pl
from jax.experimental.pallas import tpu as pltpu
from jax.sharding import PartitionSpec as P

ROWS = 16
LANES = 512
CHUNKS = (48, 80)
EPS = 1e-06
SHRINK = 1.0 / 32.0
MIB = 1 << 20
HBM = pl.BlockSpec(memory_space=pltpu.HBM)
SMEM = pl.BlockSpec(memory_space=pltpu.SMEM)
VMEM = pl.BlockSpec(memory_space=pltpu.VMEM)
ANY = pl.BlockSpec(memory_space=pl.ANY)


def sign_matrix(order):
    matrix = np.ones((1, 1), np.float32)
    while matrix.shape[0] < order:
        matrix = np.block([[matrix, matrix], [matrix, -matrix]])
    return matrix


def butterfly(parts):
    parts, half = list(parts), 1
    while half < len(parts):
        for i in range(len(parts)):
            if not i & half:
                a, b = parts[i], parts[i | half]
                parts[i], parts[i | half] = a + b, a - b
        half *= 2
    return parts


def wide(value):
    return value.astype(jnp.float32)


def narrow(value):
    return value.astype(jnp.bfloat16)


def diagonal(size):
    return lax.broadcasted_iota(jnp.int32, (size, size), 0) == lax.broadcasted_iota(jnp.int32, (size, size), 1)


def as_row(column):
    return jnp.sum(jnp.where(diagonal(column.shape[0]), column, 0.0), axis=0, keepdims=True)


def as_column(row):
    return jnp.sum(jnp.where(diagonal(row.shape[1]), row, 0.0), axis=1, keepdims=True)


def call(kernel, out_shape, operands, specs, name, limit=16, scratch=(), after=None, flops=10**10):
    body = kernel
    if after is not None:
        place = len(operands)
        operands, specs = [*operands, after], [*specs, ANY]

        def body(*refs):
            kernel(*refs[:place], *refs[place + 1 :])

    return pl.pallas_call(
        body,
        out_shape=out_shape,
        in_specs=specs,
        out_specs=jax.tree.map(lambda unused: VMEM, out_shape),
        scratch_shapes=scratch,
        compiler_params=pltpu.CompilerParams(vmem_limit_bytes=limit * MIB),
        cost_estimate=pl.CostEstimate(flops=flops, bytes_accessed=0, transcendentals=0),
        name=name,
    )(*operands)


def fetch(first, gradients_ref, held, sems):
    tiles, blocks = sems.shape
    width = held.shape[2] // blocks
    copies = []
    for i in range(tiles):
        row = []
        for p in range(blocks):
            span = pl.ds(p * width, width)
            copy = pltpu.make_async_copy(
                gradients_ref.at[pl.ds(first + i * ROWS, ROWS), span], held.at[i, :, span], sems.at[i, p]
            )
            copy.start()
            row.append(copy)
        copies.append(row)
    return copies


def reverse_bits(number, count):
    return sum((number >> i & 1) << (count - 1 - i) for i in range(count))


def outer_terms(feat_count, core, spread, tiles, store, make_sign=None):
    blocks, unused, width = spread.shape
    inner = width // feat_count
    lanes = min(LANES, inner)
    count = feat_count.bit_length() - 1
    places = [
        pl.multiple_of(jnp.where(core == 0, h, reverse_bits(h, count)) * inner, inner) for h in range(feat_count)
    ]

    @pl.loop(0, inner // lanes)
    def step(c):
        start = pl.multiple_of(c * lanes, lanes)
        for i, tile in enumerate(tiles):
            sums = []
            for h in range(feat_count):
                span = pl.ds(pl.multiple_of(places[h] + start, lanes), lanes)
                if make_sign is not None and i == 0:
                    for p in range(blocks):
                        spread[p, :, span] = make_sign(p, span)
                total = None
                for p in range(blocks):
                    piece = tile[:, pl.ds(pl.multiple_of(p * width + places[h] + start, lanes), lanes)]
                    term = wide(piece * spread[p, :, span])
                    total = term if total is None else total + term
                sums.append(total)
            for d, value in enumerate(butterfly(sums)):
                store(d, pl.ds(i * ROWS, ROWS), pl.ds(start, lanes), narrow(value))


def first_kernel(feat_count, feat_ref, core_ref, order_hbm, signs_hbm, gradients_ref, *refs):
    outs, (spread, held, sems, order, signs, mine, place, few) = refs[:feat_count], refs[feat_count:]
    order_copy = pltpu.make_async_copy(order_hbm, order, few.at[0])
    order_copy.start()
    copies = fetch(0, gradients_ref, held, sems)
    feat = feat_ref[0]
    blocks, unused, width = spread.shape
    inner = width // feat_count
    order_copy.wait()
    for b in range(order.shape[0]):
        place[order[b]] = b
    sign_copies = []
    for p in range(blocks):
        row = place[feat * blocks + p]
        sign_copies.append(pltpu.make_async_copy(signs_hbm.at[pl.ds(row, 1)], signs.at[pl.ds(p, 1)], few.at[1 + p]))
        sign_copies[-1].start()
    for copy in sign_copies:
        copy.wait()
    for h in range(feat_count):
        bits = feat & h
        odd = 0
        for shift in range(feat_count.bit_length() - 1):
            odd = odd ^ ((bits >> shift) & 1)
        span = pl.ds(h * inner, inner)
        mine[:, span] = wide(signs[:, span] * (1 - 2 * odd)) * SHRINK

    def make_sign(p, span):
        return narrow(jnp.broadcast_to(mine[pl.ds(p, 1), span], (ROWS, span.size)))

    def store(d, rows, lanes, value):
        outs[d][rows, lanes] = value

    for tile in copies:
        for copy in tile:
            copy.wait()
    tiles = [held.at[i] for i in range(held.shape[0])]
    outer_terms(feat_count, core_ref[0], spread, tiles, store, make_sign)


def first_terms(feat_count, feat, core, block_order, signs, gradients):
    rows, columns = gradients.shape
    total, width = signs.shape
    blocks = columns // width
    part = jax.ShapeDtypeStruct((rows, width // feat_count), jnp.bfloat16)
    *parts, table = call(
        functools.partial(first_kernel, feat_count),
        [part] * feat_count + [jax.ShapeDtypeStruct((blocks, ROWS, width), jnp.bfloat16)],
        [feat, core, block_order, signs, gradients],
        [SMEM, SMEM, HBM, HBM, HBM],
        "first_terms",
        flops=2 * 10**10,
        limit=7,
        scratch=[
            pltpu.VMEM((rows // ROWS, ROWS, columns), jnp.bfloat16),
            pltpu.SemaphoreType.DMA((rows // ROWS, blocks)),
            pltpu.SMEM((total,), jnp.int32),
            pltpu.VMEM((blocks, width), jnp.int32),
            pltpu.VMEM((blocks, width), jnp.float32),
            pltpu.SMEM((total,), jnp.int32),
            pltpu.SemaphoreType.DMA((1 + blocks,)),
        ],
    )
    return parts, table


def halving_places(bits):
    count = len(bits)
    numbers = [sum((d >> bit & 1) << (count - 1 - i) for i, bit in enumerate(bits)) for d in range(1 << count)]
    return [divmod(number, 1 << (count - 1)) for number in numbers]


def terms_kernel(first, places, core_ref, spread, gradients_ref, *outs):
    def store(d, rows, lanes, value):
        half, place = places[d]
        outs[half][place, rows, lanes] = value

    tiles = [gradients_ref.at[pl.ds(first + i, ROWS)] for i in range(0, outs[0].shape[1], ROWS)]
    outer_terms(len(places), core_ref[0], spread, tiles, store)


def terms(bits, core, table, gradients, first, rows, after):
    blocks, unused, width = table.shape
    feat_count = 1 << len(bits)
    columns = gradients.shape[1]
    part = jax.ShapeDtypeStruct((feat_count // 2, rows, width // feat_count), jnp.bfloat16)
    return call(
        functools.partial(terms_kernel, first, halving_places(bits)),
        [part, part],
        [core, table, gradients],
        [SMEM, VMEM, VMEM],
        "terms",
        limit=4,
        after=after,
    )


def add_parts(refs, low, high):
    total = wide(refs[0][low:high])
    for ref in refs[1:]:
        total = total + wide(ref[low:high])
    return total


def middle_kernel(low, high, *refs):
    refs[-1][...] = add_parts(refs[:-1], low, high).astype(refs[-1].dtype)


def middle(parts, low, high, after):
    return call(
        functools.partial(middle_kernel, low, high),
        jax.ShapeDtypeStruct((high - low, *parts[0].shape[1:]), parts[0].dtype),
        parts,
        [VMEM] * len(parts),
        "middle",
        limit=16,
        after=after,
    )


def combine_kernel(*refs):
    refs[-1][...] = narrow(add_parts(refs[:-1], 0, refs[-1].shape[0]))


def combine(parts, after):
    return call(
        combine_kernel,
        jax.ShapeDtypeStruct(parts[0].shape, jnp.bfloat16),
        parts,
        [VMEM] * len(parts),
        "combine",
        limit=16,
        after=after,
    )


def inner_part(scale, table, t1):
    side = table.shape[0]
    parts = butterfly(
        [
            jnp.dot(t1[:, c : c + side], table, preferred_element_type=jnp.float32)
            for c in range(0, t1.shape[1], side)
        ]
    )
    return narrow(jnp.concatenate(parts, axis=1) * scale)


def inner_table(width):
    return jnp.asarray(sign_matrix(min(256, width)), jnp.bfloat16)


def stack_kernel(feat_count, per, feat_ref, *refs):
    parts, out_ref = refs[:-1], refs[-1]
    feat = feat_ref[0]
    rows, inner = parts[0].shape
    count = rows * len(parts)
    columns = []
    for i, part in enumerate(parts):
        value = part[...]
        out_ref[pl.ds(i * rows, rows), :] = value
        columns.append(square_sums(value))
    place = lax.broadcasted_iota(jnp.int32, (count, count), 1)
    source = lax.broadcasted_iota(jnp.int32, (count, count), 0)
    share = count // feat_count
    d, left = place // share, place % share
    wanted = (left // per) * rows + (d ^ feat) * per + left % per
    norms = jnp.sum(jnp.where(source == wanted, jnp.concatenate(columns, axis=0), 0.0), axis=0, keepdims=True)
    pieces = []
    for unused in range(3):
        piece = narrow(norms)
        norms = norms - wide(piece)
        pieces.append(wide(piece))
    pieces = jnp.concatenate([*pieces, jnp.zeros((ROWS - 3, count), jnp.float32)], axis=0)
    out_ref[pl.ds(count, ROWS), pl.ds(0, count)] = narrow(pieces)
    if inner > count:
        out_ref[pl.ds(count, ROWS), pl.ds(count, inner - count)] = jnp.zeros((ROWS, inner - count), jnp.bfloat16)


def stack_targets(feat_count, per, feat, parts, after):
    rows, inner = parts[0].shape
    return call(
        functools.partial(stack_kernel, feat_count, per),
        jax.ShapeDtypeStruct((rows * len(parts) + ROWS, inner), jnp.bfloat16),
        [feat, *parts],
        [SMEM] + [VMEM] * len(parts),
        "stack_targets",
        after=after,
    )


def square_sums(value):
    value = wide(value)
    return jnp.sum(value * value, axis=1, keepdims=True)


def join_kernel(*refs):
    refs[-1][...] = narrow(add_parts(refs[:-1], 0, 1)[0])


def join(parts):
    return call(
        join_kernel,
        jax.ShapeDtypeStruct(parts[0].shape[1:], jnp.bfloat16),
        parts,
        [VMEM] * len(parts),
        "join",
    )


def gram_kernel(per, feat_ref, core_ref, mine_ref, other_ref, first_ref, *refs):
    parts, last_ref, outs, products = refs[0], refs[1], refs[2], refs[3]
    feat = feat_ref[0]
    last = narrow(add_parts(parts, 0, 1)[0])
    last_ref[...] = last
    train = jnp.concatenate([first_ref[...], last], axis=0)
    rows = train.shape[0]
    height = mine_ref.shape[0] - ROWS
    share = height // len(outs)
    target_norms = []
    for i, ref in enumerate((mine_ref, other_ref)):
        products[pl.ds(i * height, height), :] = lax.dot_general(
            ref[pl.ds(0, height), :], train, (((1,), (1,)), ((), ())), preferred_element_type=jnp.float32
        )
        pieces = wide(ref[pl.ds(height, ROWS), pl.ds(0, height)])
        target_norms.append(pieces[0:1] + pieces[1:2] + pieces[2:3])
    norms = as_row(square_sums(train))
    count = len(outs).bit_length() - 1
    for d, out in enumerate(outs):
        turned = reverse_bits(d, count)
        number = jnp.where(core_ref[0] == 0, d, turned)
        for i in range(0, 2 * share, per):
            first = pl.multiple_of((i * len(outs)) + (number ^ feat) * per, per)
            out[pl.ds(i, per), :] = products[pl.ds(first, per), :]
        straight, crossed = (
            jnp.concatenate([x[:, i * share : (i + 1) * share] for x in target_norms], axis=1) for i in (d, turned)
        )
        here = jnp.concatenate(
            [jnp.where(core_ref[0] == 0, straight, crossed), jnp.zeros((1, rows - 2 * share), jnp.float32)], axis=1
        )
        out[pl.ds(2 * share, 8), :] = jnp.concatenate([norms, here, jnp.zeros((6, rows), jnp.float32)], axis=0)


def gram(feat_count, per, feat, core, mine, other, first, parts):
    total = 2 * (mine.shape[0] - ROWS)
    unused, last_rows, inner = parts[0].shape
    rows = first.shape[0] + last_rows

    def kernel(*refs):
        split = 5 + len(parts)
        gram_kernel(per, *refs[:5], refs[5:split], refs[split], refs[split + 1 : -1], refs[-1])

    last, *outs = call(
        kernel,
        [jax.ShapeDtypeStruct((last_rows, inner), jnp.bfloat16)]
        + [jax.ShapeDtypeStruct((total // feat_count + 8, rows), jnp.float32)] * feat_count,
        [feat, core, mine, other, first, *parts],
        [SMEM, SMEM] + [VMEM] * (3 + len(parts)),
        "gram",
        scratch=[pltpu.VMEM((total, rows), jnp.float32)],
    )
    return last, outs


def inner_kernel(scale, table_ref, *refs):
    row = 0
    for ref in refs[:-1]:
        rows = ref.shape[0]
        refs[-1][pl.ds(row, rows), :] = inner_part(scale, table_ref[...], ref[...])
        row += rows


def inner_transform(scale, table, chunks):
    rows = sum(chunk.shape[0] for chunk in chunks)
    return call(
        functools.partial(inner_kernel, scale),
        jax.ShapeDtypeStruct((rows, chunks[0].shape[1]), jnp.bfloat16),
        [table, *chunks],
        [VMEM] * (1 + len(chunks)),
        "inner_transform",
        limit=16,
    )


def finish_kernel(mean_scale, per, ex_ref, projected_ref, *refs):
    parts, (features_ref, cosines_ref) = refs[:-2], refs[-2:]
    count = cosines_ref.shape[0]
    share = count // 2
    sums = parts[0][...]
    for part in parts[1:]:
        sums = sums + part[...]
    train_scale = lax.rsqrt(sums[count : count + 1] * mean_scale + EPS)
    target_scale = lax.rsqrt(sums[count + 1 : count + 2, :count] * mean_scale + EPS)
    cosines = sums[:count] * train_scale * as_column(target_scale) * mean_scale
    for i in range(count // per):
        group = ex_ref[0] ^ (i * 2 if i * per < share else i * 2 - count // per + 1)
        cosines_ref[pl.ds(pl.multiple_of(group * per, per), per), :] = cosines[i * per : (i + 1) * per]
    features_ref[...] = narrow(wide(projected_ref[...]) * as_column(train_scale))


def finish(mean_scale, per, ex, projected, parts):
    return call(
        functools.partial(finish_kernel, mean_scale, per),
        [
            jax.ShapeDtypeStruct(projected.shape, jnp.bfloat16),
            jax.ShapeDtypeStruct((parts[0].shape[0] - 8, projected.shape[0]), jnp.float32),
        ],
        [ex, projected, *parts],
        [SMEM] + [VMEM] * (1 + len(parts)),
        "finish",
    )


def swap(value, axis, distance):
    return lax.ppermute(value, axis, [(i, i ^ distance) for i in range(lax.axis_size(axis))])


def local(train_grads, target_grads, signs, block_order):
    train_grads, target_grads, signs, block_order = (
        pltpu.with_memory_space_constraint(value, pltpu.HBM)
        for value in (train_grads, target_grads, signs, block_order)
    )
    train_grads = pltpu.with_memory_space_constraint(train_grads, pltpu.VMEM)
    block_total, width = signs.shape
    feat_count = lax.axis_size("feat")
    groups = lax.axis_size("ex")
    feat = lax.axis_index("feat").astype(jnp.int32).reshape(1)
    ex = lax.axis_index("ex").astype(jnp.int32)
    train_rows, target_rows = train_grads.shape[0], target_grads.shape[0]
    per = target_rows // feat_count
    inner = width // feat_count
    mean_scale = 1.0 / (block_total * width * feat_count * SHRINK**2)
    scale = 1.0 / (math.sqrt(block_total * width) * SHRINK)
    table256 = inner_table(inner)
    bits = list(range(feat_count.bit_length() - 1))
    assert sum(CHUNKS) == train_rows

    core = (ex % 2).reshape(1)

    def turn(value, d):
        other = reverse_bits(d, len(bits))
        pairs = [
            (f * groups + e, (f ^ (d if e % 2 == 0 else other)) * groups + e)
            for f in range(feat_count)
            for e in range(groups)
        ]
        return lax.ppermute(value, ("feat", "ex"), pairs)

    target_parts, table = first_terms(feat_count, feat, core, block_order, signs, target_grads)
    own = pltpu.with_memory_space_constraint(target_parts[0], pltpu.VMEM)
    got = [own] + [turn(target_parts[d], d) for d in range(1, feat_count)]

    orders = [bits if i % 2 == 0 else bits[::-1] for i in range(len(CHUNKS))]
    firsts = [sum(CHUNKS[:i]) for i in range(len(CHUNKS))]

    def start(i, after):
        keep, send = terms(orders[i], core, table, train_grads, firsts[i], CHUNKS[i], after)
        return [keep, turn(send, 1 << orders[i][0])], send

    def proceed(order, parts, after):
        for bit in order[1:]:
            high = parts[-1].shape[0]
            send = after = middle(parts, high // 2, high, after)
            parts = [*parts, turn(send, 1 << bit)]
        return parts, after

    state = [None] * len(CHUNKS)
    state[0], mark = start(0, None)
    state[1], mark = start(1, mark)
    own = combine(got, mark)
    around = [own] + [swap(own, "ex", d) for d in range(2, groups, 2)]
    state[0], mark = proceed(orders[0], state[0], own)
    state[1], mark = proceed(orders[1], state[1], mark)
    mine = stack_targets(feat_count, per, feat, around, mark)
    other = swap(mine, "ex", 1)
    first = join(state[0])
    last, sums = gram(feat_count, per, feat, core, mine, other, first, state[1])
    far = sorted(range(1, feat_count), key=lambda d: -d.bit_count())
    sums = [sums[0]] + [turn(sums[d], d) for d in far]
    projected = inner_transform(scale, table256, [first, last])
    features, cosines = finish(mean_scale, per, ex.reshape(1), projected, sums)
    return features, cosines.reshape(groups, per, train_rows).transpose(2, 0, 1)


def solution(mesh):
    placed = (P("ex", "feat"), P("ex", "feat"), P(), P())
    return jax.shard_map(
        local,
        mesh=mesh,
        in_specs=placed,
        out_specs=(P("ex", "feat"), P("ex", None, "feat")),
        check_vma=False,
    )
```

```python
import functools
import math

import jax
import jax.numpy as jnp
import numpy as np
from jax import lax
from jax.experimental import pallas as pl
from jax.experimental.pallas import tpu as pltpu
from jax.sharding import PartitionSpec as P

ROWS = 16
LANES = 512
CHUNKS = (48, 80)
EPS = 1e-06
SHRINK = 1.0 / 32.0
MIB = 1 << 20
HBM = pl.BlockSpec(memory_space=pltpu.HBM)
SMEM = pl.BlockSpec(memory_space=pltpu.SMEM)
VMEM = pl.BlockSpec(memory_space=pltpu.VMEM)
ANY = pl.BlockSpec(memory_space=pl.ANY)


def sign_matrix(order):
    matrix = np.ones((1, 1), np.float32)
    while matrix.shape[0] < order:
        matrix = np.block([[matrix, matrix], [matrix, -matrix]])
    return matrix


def butterfly(parts):
    parts, half = list(parts), 1
    while half < len(parts):
        for i in range(len(parts)):
            if not i & half:
                a, b = parts[i], parts[i | half]
                parts[i], parts[i | half] = a + b, a - b
        half *= 2
    return parts


def wide(value):
    return value.astype(jnp.float32)


def narrow(value):
    return value.astype(jnp.bfloat16)


def diagonal(size):
    return lax.broadcasted_iota(jnp.int32, (size, size), 0) == lax.broadcasted_iota(jnp.int32, (size, size), 1)


def as_row(column):
    return jnp.sum(jnp.where(diagonal(column.shape[0]), column, 0.0), axis=0, keepdims=True)


def as_column(row):
    return jnp.sum(jnp.where(diagonal(row.shape[1]), row, 0.0), axis=1, keepdims=True)


def call(kernel, out_shape, operands, specs, name, limit=16, scratch=(), after=None, flops=10**10):
    body = kernel
    if after is not None:
        place = len(operands)
        operands, specs = [*operands, after], [*specs, ANY]

        def body(*refs):
            kernel(*refs[:place], *refs[place + 1 :])

    return pl.pallas_call(
        body,
        out_shape=out_shape,
        in_specs=specs,
        out_specs=jax.tree.map(lambda unused: VMEM, out_shape),
        scratch_shapes=scratch,
        compiler_params=pltpu.CompilerParams(vmem_limit_bytes=limit * MIB),
        cost_estimate=pl.CostEstimate(flops=flops, bytes_accessed=0, transcendentals=0),
        name=name,
    )(*operands)


def fetch(first, gradients_ref, held, sems):
    tiles, blocks = sems.shape
    width = held.shape[2] // blocks
    copies = []
    for i in range(tiles):
        row = []
        for p in range(blocks):
            span = pl.ds(p * width, width)
            copy = pltpu.make_async_copy(
                gradients_ref.at[pl.ds(first + i * ROWS, ROWS), span], held.at[i, :, span], sems.at[i, p]
            )
            copy.start()
            row.append(copy)
        copies.append(row)
    return copies


def reverse_bits(number, count):
    return sum((number >> i & 1) << (count - 1 - i) for i in range(count))


def outer_terms(feat_count, core, spread, tiles, store, make_sign=None):
    blocks, unused, width = spread.shape
    inner = width // feat_count
    lanes = min(LANES, inner)
    count = feat_count.bit_length() - 1
    places = [
        pl.multiple_of(jnp.where(core == 0, h, reverse_bits(h, count)) * inner, inner) for h in range(feat_count)
    ]

    @pl.loop(0, inner // lanes)
    def step(c):
        start = pl.multiple_of(c * lanes, lanes)
        for i, tile in enumerate(tiles):
            sums = []
            for h in range(feat_count):
                span = pl.ds(pl.multiple_of(places[h] + start, lanes), lanes)
                if make_sign is not None and i == 0:
                    for p in range(blocks):
                        spread[p, :, span] = make_sign(p, span)
                total = None
                for p in range(0, blocks, 2):
                    pair = [
                        tile[:, pl.ds(pl.multiple_of(q * width + places[h] + start, lanes), lanes)] * spread[q, :, span]
                        for q in range(p, min(p + 2, blocks))
                    ]
                    term = wide(sum(pair[1:], pair[0]))
                    total = term if total is None else total + term
                sums.append(total)
            for d, value in enumerate(butterfly(sums)):
                store(d, pl.ds(i * ROWS, ROWS), pl.ds(start, lanes), narrow(value))


def first_kernel(feat_count, feat_ref, core_ref, order_hbm, signs_hbm, gradients_ref, *refs):
    outs, (spread, held, sems, order, signs, mine, place, few) = refs[:feat_count], refs[feat_count:]
    order_copy = pltpu.make_async_copy(order_hbm, order, few.at[0])
    order_copy.start()
    copies = fetch(0, gradients_ref, held, sems)
    feat = feat_ref[0]
    blocks, unused, width = spread.shape
    inner = width // feat_count
    order_copy.wait()
    for b in range(order.shape[0]):
        place[order[b]] = b
    sign_copies = []
    for p in range(blocks):
        row = place[feat * blocks + p]
        sign_copies.append(pltpu.make_async_copy(signs_hbm.at[pl.ds(row, 1)], signs.at[pl.ds(p, 1)], few.at[1 + p]))
        sign_copies[-1].start()
    for copy in sign_copies:
        copy.wait()
    for h in range(feat_count):
        bits = feat & h
        odd = 0
        for shift in range(feat_count.bit_length() - 1):
            odd = odd ^ ((bits >> shift) & 1)
        span = pl.ds(h * inner, inner)
        mine[:, span] = wide(signs[:, span] * (1 - 2 * odd)) * SHRINK

    def make_sign(p, span):
        return narrow(jnp.broadcast_to(mine[pl.ds(p, 1), span], (ROWS, span.size)))

    def store(d, rows, lanes, value):
        outs[d][rows, lanes] = value

    for tile in copies:
        for copy in tile:
            copy.wait()
    tiles = [held.at[i] for i in range(held.shape[0])]
    outer_terms(feat_count, core_ref[0], spread, tiles, store, make_sign)


def first_terms(feat_count, feat, core, block_order, signs, gradients):
    rows, columns = gradients.shape
    total, width = signs.shape
    blocks = columns // width
    part = jax.ShapeDtypeStruct((rows, width // feat_count), jnp.bfloat16)
    *parts, table = call(
        functools.partial(first_kernel, feat_count),
        [part] * feat_count + [jax.ShapeDtypeStruct((blocks, ROWS, width), jnp.bfloat16)],
        [feat, core, block_order, signs, gradients],
        [SMEM, SMEM, HBM, HBM, HBM],
        "first_terms",
        flops=2 * 10**10,
        limit=7,
        scratch=[
            pltpu.VMEM((rows // ROWS, ROWS, columns), jnp.bfloat16),
            pltpu.SemaphoreType.DMA((rows // ROWS, blocks)),
            pltpu.SMEM((total,), jnp.int32),
            pltpu.VMEM((blocks, width), jnp.int32),
            pltpu.VMEM((blocks, width), jnp.float32),
            pltpu.SMEM((total,), jnp.int32),
            pltpu.SemaphoreType.DMA((1 + blocks,)),
        ],
    )
    return parts, table


def halving_places(bits):
    count = len(bits)
    numbers = [sum((d >> bit & 1) << (count - 1 - i) for i, bit in enumerate(bits)) for d in range(1 << count)]
    return [divmod(number, 1 << (count - 1)) for number in numbers]


def terms_kernel(first, places, core_ref, spread, gradients_ref, *outs):
    def store(d, rows, lanes, value):
        half, place = places[d]
        outs[half][place, rows, lanes] = value

    tiles = [gradients_ref.at[pl.ds(first + i, ROWS)] for i in range(0, outs[0].shape[1], ROWS)]
    outer_terms(len(places), core_ref[0], spread, tiles, store)


def terms(bits, core, table, gradients, first, rows, after):
    blocks, unused, width = table.shape
    feat_count = 1 << len(bits)
    columns = gradients.shape[1]
    part = jax.ShapeDtypeStruct((feat_count // 2, rows, width // feat_count), jnp.bfloat16)
    return call(
        functools.partial(terms_kernel, first, halving_places(bits)),
        [part, part],
        [core, table, gradients],
        [SMEM, VMEM, VMEM],
        "terms",
        limit=4,
        after=after,
    )


def add_parts(refs, low, high):
    total = wide(refs[0][low:high])
    for ref in refs[1:]:
        total = total + wide(ref[low:high])
    return total


def middle_kernel(low, high, *refs):
    refs[-1][...] = add_parts(refs[:-1], low, high).astype(refs[-1].dtype)


def middle(parts, low, high, after):
    return call(
        functools.partial(middle_kernel, low, high),
        jax.ShapeDtypeStruct((high - low, *parts[0].shape[1:]), parts[0].dtype),
        parts,
        [VMEM] * len(parts),
        "middle",
        limit=16,
        after=after,
    )


def combine_kernel(*refs):
    refs[-1][...] = narrow(add_parts(refs[:-1], 0, refs[-1].shape[0]))


def combine(parts, after):
    return call(
        combine_kernel,
        jax.ShapeDtypeStruct(parts[0].shape, jnp.bfloat16),
        parts,
        [VMEM] * len(parts),
        "combine",
        limit=16,
        after=after,
    )


def inner_part(scale, table, t1):
    side = table.shape[0]
    parts = butterfly(
        [
            jnp.dot(t1[:, c : c + side], table, preferred_element_type=jnp.float32)
            for c in range(0, t1.shape[1], side)
        ]
    )
    return narrow(jnp.concatenate(parts, axis=1) * scale)


def inner_table(width):
    return jnp.asarray(sign_matrix(min(256, width)), jnp.bfloat16)


def stack_kernel(feat_count, per, feat_ref, *refs):
    parts, out_ref = refs[:-1], refs[-1]
    feat = feat_ref[0]
    rows, inner = parts[0].shape
    count = rows * len(parts)
    columns = []
    for i, part in enumerate(parts):
        value = part[...]
        out_ref[pl.ds(i * rows, rows), :] = value
        columns.append(square_sums(value))
    place = lax.broadcasted_iota(jnp.int32, (count, count), 1)
    source = lax.broadcasted_iota(jnp.int32, (count, count), 0)
    share = count // feat_count
    d, left = place // share, place % share
    wanted = (left // per) * rows + (d ^ feat) * per + left % per
    norms = jnp.sum(jnp.where(source == wanted, jnp.concatenate(columns, axis=0), 0.0), axis=0, keepdims=True)
    pieces = []
    for unused in range(3):
        piece = narrow(norms)
        norms = norms - wide(piece)
        pieces.append(wide(piece))
    pieces = jnp.concatenate([*pieces, jnp.zeros((ROWS - 3, count), jnp.float32)], axis=0)
    out_ref[pl.ds(count, ROWS), pl.ds(0, count)] = narrow(pieces)
    if inner > count:
        out_ref[pl.ds(count, ROWS), pl.ds(count, inner - count)] = jnp.zeros((ROWS, inner - count), jnp.bfloat16)


def stack_targets(feat_count, per, feat, parts, after):
    rows, inner = parts[0].shape
    return call(
        functools.partial(stack_kernel, feat_count, per),
        jax.ShapeDtypeStruct((rows * len(parts) + ROWS, inner), jnp.bfloat16),
        [feat, *parts],
        [SMEM] + [VMEM] * len(parts),
        "stack_targets",
        after=after,
    )


def square_sums(value):
    value = wide(value)
    return jnp.sum(value * value, axis=1, keepdims=True)


def join_kernel(*refs):
    refs[-1][...] = narrow(add_parts(refs[:-1], 0, 1)[0])


def join(parts):
    return call(
        join_kernel,
        jax.ShapeDtypeStruct(parts[0].shape[1:], jnp.bfloat16),
        parts,
        [VMEM] * len(parts),
        "join",
    )


def gram_kernel(per, feat_ref, core_ref, mine_ref, other_ref, first_ref, *refs):
    parts, last_ref, outs, products = refs[0], refs[1], refs[2], refs[3]
    feat = feat_ref[0]
    last = narrow(add_parts(parts, 0, 1)[0])
    last_ref[...] = last
    train = jnp.concatenate([first_ref[...], last], axis=0)
    rows = train.shape[0]
    height = mine_ref.shape[0] - ROWS
    share = height // len(outs)
    target_norms = []
    for i, ref in enumerate((mine_ref, other_ref)):
        products[pl.ds(i * height, height), :] = lax.dot_general(
            ref[pl.ds(0, height), :], train, (((1,), (1,)), ((), ())), preferred_element_type=jnp.float32
        )
        pieces = wide(ref[pl.ds(height, ROWS), pl.ds(0, height)])
        target_norms.append(pieces[0:1] + pieces[1:2] + pieces[2:3])
    norms = as_row(square_sums(train))
    count = len(outs).bit_length() - 1
    for d, out in enumerate(outs):
        turned = reverse_bits(d, count)
        number = jnp.where(core_ref[0] == 0, d, turned)
        for i in range(0, 2 * share, per):
            first = pl.multiple_of((i * len(outs)) + (number ^ feat) * per, per)
            out[pl.ds(i, per), :] = products[pl.ds(first, per), :]
        straight, crossed = (
            jnp.concatenate([x[:, i * share : (i + 1) * share] for x in target_norms], axis=1) for i in (d, turned)
        )
        here = jnp.concatenate(
            [jnp.where(core_ref[0] == 0, straight, crossed), jnp.zeros((1, rows - 2 * share), jnp.float32)], axis=1
        )
        out[pl.ds(2 * share, 8), :] = jnp.concatenate([norms, here, jnp.zeros((6, rows), jnp.float32)], axis=0)


def gram(feat_count, per, feat, core, mine, other, first, parts):
    total = 2 * (mine.shape[0] - ROWS)
    unused, last_rows, inner = parts[0].shape
    rows = first.shape[0] + last_rows

    def kernel(*refs):
        split = 5 + len(parts)
        gram_kernel(per, *refs[:5], refs[5:split], refs[split], refs[split + 1 : -1], refs[-1])

    last, *outs = call(
        kernel,
        [jax.ShapeDtypeStruct((last_rows, inner), jnp.bfloat16)]
        + [jax.ShapeDtypeStruct((total // feat_count + 8, rows), jnp.float32)] * feat_count,
        [feat, core, mine, other, first, *parts],
        [SMEM, SMEM] + [VMEM] * (3 + len(parts)),
        "gram",
        scratch=[pltpu.VMEM((total, rows), jnp.float32)],
    )
    return last, outs


def inner_kernel(scale, table_ref, *refs):
    row = 0
    for ref in refs[:-1]:
        rows = ref.shape[0]
        refs[-1][pl.ds(row, rows), :] = inner_part(scale, table_ref[...], ref[...])
        row += rows


def inner_transform(scale, table, chunks):
    rows = sum(chunk.shape[0] for chunk in chunks)
    return call(
        functools.partial(inner_kernel, scale),
        jax.ShapeDtypeStruct((rows, chunks[0].shape[1]), jnp.bfloat16),
        [table, *chunks],
        [VMEM] * (1 + len(chunks)),
        "inner_transform",
        limit=16,
    )


def finish_kernel(mean_scale, per, ex_ref, projected_ref, *refs):
    parts, (features_ref, cosines_ref) = refs[:-2], refs[-2:]
    count = cosines_ref.shape[0]
    share = count // 2
    sums = parts[0][...]
    for part in parts[1:]:
        sums = sums + part[...]
    train_scale = lax.rsqrt(sums[count : count + 1] * mean_scale + EPS)
    target_scale = lax.rsqrt(sums[count + 1 : count + 2, :count] * mean_scale + EPS)
    cosines = sums[:count] * train_scale * as_column(target_scale) * mean_scale
    for i in range(count // per):
        group = ex_ref[0] ^ (i * 2 if i * per < share else i * 2 - count // per + 1)
        cosines_ref[pl.ds(pl.multiple_of(group * per, per), per), :] = cosines[i * per : (i + 1) * per]
    features_ref[...] = narrow(wide(projected_ref[...]) * as_column(train_scale))


def finish(mean_scale, per, ex, projected, parts):
    return call(
        functools.partial(finish_kernel, mean_scale, per),
        [
            jax.ShapeDtypeStruct(projected.shape, jnp.bfloat16),
            jax.ShapeDtypeStruct((parts[0].shape[0] - 8, projected.shape[0]), jnp.float32),
        ],
        [ex, projected, *parts],
        [SMEM] + [VMEM] * (1 + len(parts)),
        "finish",
    )


def swap(value, axis, distance):
    return lax.ppermute(value, axis, [(i, i ^ distance) for i in range(lax.axis_size(axis))])


def local(train_grads, target_grads, signs, block_order):
    train_grads, target_grads, signs, block_order = (
        pltpu.with_memory_space_constraint(value, pltpu.HBM)
        for value in (train_grads, target_grads, signs, block_order)
    )
    train_grads = pltpu.with_memory_space_constraint(train_grads, pltpu.VMEM)
    block_total, width = signs.shape
    feat_count = lax.axis_size("feat")
    groups = lax.axis_size("ex")
    feat = lax.axis_index("feat").astype(jnp.int32).reshape(1)
    ex = lax.axis_index("ex").astype(jnp.int32)
    train_rows, target_rows = train_grads.shape[0], target_grads.shape[0]
    per = target_rows // feat_count
    inner = width // feat_count
    mean_scale = 1.0 / (block_total * width * feat_count * SHRINK**2)
    scale = 1.0 / (math.sqrt(block_total * width) * SHRINK)
    table256 = inner_table(inner)
    bits = list(range(feat_count.bit_length() - 1))
    assert sum(CHUNKS) == train_rows

    core = (ex % 2).reshape(1)

    def turn(value, d):
        other = reverse_bits(d, len(bits))
        pairs = [
            (f * groups + e, (f ^ (d if e % 2 == 0 else other)) * groups + e)
            for f in range(feat_count)
            for e in range(groups)
        ]
        return lax.ppermute(value, ("feat", "ex"), pairs)

    target_parts, table = first_terms(feat_count, feat, core, block_order, signs, target_grads)
    own = pltpu.with_memory_space_constraint(target_parts[0], pltpu.VMEM)
    got = [own] + [turn(target_parts[d], d) for d in range(1, feat_count)]

    orders = [bits if i % 2 == 0 else bits[::-1] for i in range(len(CHUNKS))]
    firsts = [sum(CHUNKS[:i]) for i in range(len(CHUNKS))]

    def start(i, after):
        keep, send = terms(orders[i], core, table, train_grads, firsts[i], CHUNKS[i], after)
        return [keep, turn(send, 1 << orders[i][0])], send

    def proceed(order, parts, after):
        for bit in order[1:]:
            high = parts[-1].shape[0]
            send = after = middle(parts, high // 2, high, after)
            parts = [*parts, turn(send, 1 << bit)]
        return parts, after

    state = [None] * len(CHUNKS)
    state[0], mark = start(0, None)
    state[1], mark = start(1, mark)
    own = combine(got, mark)
    around = [own] + [swap(own, "ex", d) for d in range(2, groups, 2)]
    state[0], mark = proceed(orders[0], state[0], own)
    state[1], mark = proceed(orders[1], state[1], mark)
    mine = stack_targets(feat_count, per, feat, around, mark)
    other = swap(mine, "ex", 1)
    first = join(state[0])
    last, sums = gram(feat_count, per, feat, core, mine, other, first, state[1])
    far = sorted(range(1, feat_count), key=lambda d: -d.bit_count())
    sums = [sums[0]] + [turn(sums[d], d) for d in far]
    projected = inner_transform(scale, table256, [first, last])
    features, cosines = finish(mean_scale, per, ex.reshape(1), projected, sums)
    return features, cosines.reshape(groups, per, train_rows).transpose(2, 0, 1)


def solution(mesh):
    placed = (P("ex", "feat"), P("ex", "feat"), P(), P())
    return jax.shard_map(
        local,
        mesh=mesh,
        in_specs=placed,
        out_specs=(P("ex", "feat"), P("ex", None, "feat")),
        check_vma=False,
    )
```

```python
import functools
import math

import jax
import jax.numpy as jnp
import numpy as np
from jax import lax
from jax.experimental import pallas as pl
from jax.experimental.pallas import tpu as pltpu
from jax.sharding import PartitionSpec as P

ROWS = 16
LANES = 512
CHUNKS = (48, 80)
EPS = 1e-06
SHRINK = 1.0 / 32.0
MIB = 1 << 20
HBM = pl.BlockSpec(memory_space=pltpu.HBM)
SMEM = pl.BlockSpec(memory_space=pltpu.SMEM)
VMEM = pl.BlockSpec(memory_space=pltpu.VMEM)
ANY = pl.BlockSpec(memory_space=pl.ANY)


def sign_matrix(order):
    matrix = np.ones((1, 1), np.float32)
    while matrix.shape[0] < order:
        matrix = np.block([[matrix, matrix], [matrix, -matrix]])
    return matrix


def butterfly(parts):
    parts, half = list(parts), 1
    while half < len(parts):
        for i in range(len(parts)):
            if not i & half:
                a, b = parts[i], parts[i | half]
                parts[i], parts[i | half] = a + b, a - b
        half *= 2
    return parts


def wide(value):
    return value.astype(jnp.float32)


def narrow(value):
    return value.astype(jnp.bfloat16)


def diagonal(size):
    return lax.broadcasted_iota(jnp.int32, (size, size), 0) == lax.broadcasted_iota(jnp.int32, (size, size), 1)


def as_row(column):
    return jnp.sum(jnp.where(diagonal(column.shape[0]), column, 0.0), axis=0, keepdims=True)


def as_column(row):
    return jnp.sum(jnp.where(diagonal(row.shape[1]), row, 0.0), axis=1, keepdims=True)


def call(kernel, out_shape, operands, specs, name, limit=16, scratch=(), after=None, flops=10**10):
    body = kernel
    if after is not None:
        place = len(operands)
        operands, specs = [*operands, after], [*specs, ANY]

        def body(*refs):
            kernel(*refs[:place], *refs[place + 1 :])

    return pl.pallas_call(
        body,
        out_shape=out_shape,
        in_specs=specs,
        out_specs=jax.tree.map(lambda unused: VMEM, out_shape),
        scratch_shapes=scratch,
        compiler_params=pltpu.CompilerParams(vmem_limit_bytes=limit * MIB),
        cost_estimate=pl.CostEstimate(flops=flops, bytes_accessed=0, transcendentals=0),
        name=name,
    )(*operands)


def fetch(first, gradients_ref, held, sems):
    tiles, blocks = sems.shape
    width = held.shape[2] // blocks
    copies = []
    for i in range(tiles):
        row = []
        for p in range(blocks):
            span = pl.ds(p * width, width)
            copy = pltpu.make_async_copy(
                gradients_ref.at[pl.ds(first + i * ROWS, ROWS), span], held.at[i, :, span], sems.at[i, p]
            )
            copy.start()
            row.append(copy)
        copies.append(row)
    return copies


def reverse_bits(number, count):
    return sum((number >> i & 1) << (count - 1 - i) for i in range(count))


def outer_terms(feat_count, core, spread, tiles, store, make_sign=None):
    blocks, unused, width = spread.shape
    inner = width // feat_count
    lanes = min(LANES, inner)
    count = feat_count.bit_length() - 1
    places = [
        pl.multiple_of(jnp.where(core == 0, h, reverse_bits(h, count)) * inner, inner) for h in range(feat_count)
    ]

    @pl.loop(0, inner // lanes)
    def step(c):
        start = pl.multiple_of(c * lanes, lanes)
        for i, tile in enumerate(tiles):
            sums = []
            for h in range(feat_count):
                span = pl.ds(pl.multiple_of(places[h] + start, lanes), lanes)
                if make_sign is not None and i == 0:
                    for p in range(blocks):
                        spread[p, :, span] = make_sign(p, span)
                total = None
                for p in range(0, blocks, 2):
                    pair = [
                        tile[:, pl.ds(pl.multiple_of(q * width + places[h] + start, lanes), lanes)] * spread[q, :, span]
                        for q in range(p, min(p + 2, blocks))
                    ]
                    term = wide(sum(pair[1:], pair[0]))
                    total = term if total is None else total + term
                sums.append(total)
            for d, value in enumerate(butterfly(sums)):
                store(d, pl.ds(i * ROWS, ROWS), pl.ds(start, lanes), narrow(value))


def first_kernel(feat_count, feat_ref, core_ref, order_hbm, signs_hbm, gradients_ref, *refs):
    outs, (spread, held, sems, order, signs, mine, place, few) = refs[:feat_count], refs[feat_count:]
    order_copy = pltpu.make_async_copy(order_hbm, order, few.at[0])
    order_copy.start()
    copies = fetch(0, gradients_ref, held, sems)
    feat = feat_ref[0]
    blocks, unused, width = spread.shape
    inner = width // feat_count
    order_copy.wait()
    for b in range(order.shape[0]):
        place[order[b]] = b
    sign_copies = []
    for p in range(blocks):
        row = place[feat * blocks + p]
        sign_copies.append(pltpu.make_async_copy(signs_hbm.at[pl.ds(row, 1)], signs.at[pl.ds(p, 1)], few.at[1 + p]))
        sign_copies[-1].start()
    for copy in sign_copies:
        copy.wait()
    for h in range(feat_count):
        bits = feat & h
        odd = 0
        for shift in range(feat_count.bit_length() - 1):
            odd = odd ^ ((bits >> shift) & 1)
        span = pl.ds(h * inner, inner)
        mine[:, span] = wide(signs[:, span] * (1 - 2 * odd)) * SHRINK

    def make_sign(p, span):
        return narrow(jnp.broadcast_to(mine[pl.ds(p, 1), span], (ROWS, span.size)))

    def store(d, rows, lanes, value):
        outs[d][rows, lanes] = value

    for tile in copies:
        for copy in tile:
            copy.wait()
    tiles = [held.at[i] for i in range(held.shape[0])]
    outer_terms(feat_count, core_ref[0], spread, tiles, store, make_sign)


def first_terms(feat_count, feat, core, block_order, signs, gradients):
    rows, columns = gradients.shape
    total, width = signs.shape
    blocks = columns // width
    part = jax.ShapeDtypeStruct((rows, width // feat_count), jnp.bfloat16)
    *parts, table = call(
        functools.partial(first_kernel, feat_count),
        [part] * feat_count + [jax.ShapeDtypeStruct((blocks, ROWS, width), jnp.bfloat16)],
        [feat, core, block_order, signs, gradients],
        [SMEM, SMEM, HBM, HBM, HBM],
        "first_terms",
        flops=2 * 10**10,
        limit=7,
        scratch=[
            pltpu.VMEM((rows // ROWS, ROWS, columns), jnp.bfloat16),
            pltpu.SemaphoreType.DMA((rows // ROWS, blocks)),
            pltpu.SMEM((total,), jnp.int32),
            pltpu.VMEM((blocks, width), jnp.int32),
            pltpu.VMEM((blocks, width), jnp.float32),
            pltpu.SMEM((total,), jnp.int32),
            pltpu.SemaphoreType.DMA((1 + blocks,)),
        ],
    )
    return parts, table


def halving_places(bits):
    count = len(bits)
    numbers = [sum((d >> bit & 1) << (count - 1 - i) for i, bit in enumerate(bits)) for d in range(1 << count)]
    return [divmod(number, 1 << (count - 1)) for number in numbers]


def terms_kernel(first, places, core_ref, spread, gradients_ref, *outs):
    def store(d, rows, lanes, value):
        half, place = places[d]
        outs[half][place, rows, lanes] = value

    tiles = [gradients_ref.at[pl.ds(first + i, ROWS)] for i in range(0, outs[0].shape[1], ROWS)]
    outer_terms(len(places), core_ref[0], spread, tiles, store)


def terms(bits, core, table, gradients, first, rows, after):
    blocks, unused, width = table.shape
    feat_count = 1 << len(bits)
    columns = gradients.shape[1]
    part = jax.ShapeDtypeStruct((feat_count // 2, rows, width // feat_count), jnp.bfloat16)
    return call(
        functools.partial(terms_kernel, first, halving_places(bits)),
        [part, part],
        [core, table, gradients],
        [SMEM, VMEM, VMEM],
        "terms",
        limit=4,
        after=after,
    )


def add_parts(refs, low, high):
    total = wide(refs[0][low:high])
    for ref in refs[1:]:
        total = total + wide(ref[low:high])
    return total


def middle_kernel(low, high, *refs):
    refs[-1][...] = add_parts(refs[:-1], low, high).astype(refs[-1].dtype)


def middle(parts, low, high, after):
    return call(
        functools.partial(middle_kernel, low, high),
        jax.ShapeDtypeStruct((high - low, *parts[0].shape[1:]), parts[0].dtype),
        parts,
        [VMEM] * len(parts),
        "middle",
        limit=16,
        after=after,
    )


def combine_kernel(*refs):
    refs[-1][...] = narrow(add_parts(refs[:-1], 0, refs[-1].shape[0]))


def combine(parts, after):
    return call(
        combine_kernel,
        jax.ShapeDtypeStruct(parts[0].shape, jnp.bfloat16),
        parts,
        [VMEM] * len(parts),
        "combine",
        limit=16,
        after=after,
    )


def inner_part(scale, table, t1):
    side = table.shape[0]
    parts = butterfly(
        [
            jnp.dot(t1[:, c : c + side], table, preferred_element_type=jnp.float32)
            for c in range(0, t1.shape[1], side)
        ]
    )
    return narrow(jnp.concatenate(parts, axis=1) * scale)


def inner_table(width):
    return jnp.asarray(sign_matrix(min(256, width)), jnp.bfloat16)


def stack_kernel(feat_count, per, feat_ref, *refs):
    parts, out_ref = refs[:-1], refs[-1]
    feat = feat_ref[0]
    rows, inner = parts[0].shape
    count = rows * len(parts)
    columns = []
    for i, part in enumerate(parts):
        value = part[...]
        out_ref[pl.ds(i * rows, rows), :] = value
        columns.append(square_sums(value))
    place = lax.broadcasted_iota(jnp.int32, (count, count), 1)
    source = lax.broadcasted_iota(jnp.int32, (count, count), 0)
    share = count // feat_count
    d, left = place // share, place % share
    wanted = (left // per) * rows + (d ^ feat) * per + left % per
    norms = jnp.sum(jnp.where(source == wanted, jnp.concatenate(columns, axis=0), 0.0), axis=0, keepdims=True)
    pieces = []
    for unused in range(3):
        piece = narrow(norms)
        norms = norms - wide(piece)
        pieces.append(wide(piece))
    pieces = jnp.concatenate([*pieces, jnp.zeros((ROWS - 3, count), jnp.float32)], axis=0)
    out_ref[pl.ds(count, ROWS), pl.ds(0, count)] = narrow(pieces)
    if inner > count:
        out_ref[pl.ds(count, ROWS), pl.ds(count, inner - count)] = jnp.zeros((ROWS, inner - count), jnp.bfloat16)


def stack_targets(feat_count, per, feat, parts, after):
    rows, inner = parts[0].shape
    return call(
        functools.partial(stack_kernel, feat_count, per),
        jax.ShapeDtypeStruct((rows * len(parts) + ROWS, inner), jnp.bfloat16),
        [feat, *parts],
        [SMEM] + [VMEM] * len(parts),
        "stack_targets",
        after=after,
    )


def pieces_of(row):
    pieces = []
    for unused in range(3):
        piece = wide(narrow(row))
        row = row - piece
        pieces.append(piece)
    return pieces


def square_sums(value):
    value = wide(value)
    return jnp.sum(value * value, axis=1, keepdims=True)


def join_kernel(*refs):
    refs[-1][...] = narrow(add_parts(refs[:-1], 0, 1)[0])


def join(parts):
    return call(
        join_kernel,
        jax.ShapeDtypeStruct(parts[0].shape[1:], jnp.bfloat16),
        parts,
        [VMEM] * len(parts),
        "join",
    )


def gram_kernel(per, feat_ref, core_ref, mine_ref, other_ref, first_ref, *refs):
    parts, last_ref, outs, products = refs[0], refs[1], refs[2], refs[3]
    feat = feat_ref[0]
    last = narrow(add_parts(parts, 0, 1)[0])
    last_ref[...] = last
    train = jnp.concatenate([first_ref[...], last], axis=0)
    rows = train.shape[0]
    height = mine_ref.shape[0] - ROWS
    share = height // len(outs)
    target_norms = []
    for i, ref in enumerate((mine_ref, other_ref)):
        products[pl.ds(i * height, height), :] = lax.dot_general(
            ref[pl.ds(0, height), :], train, (((1,), (1,)), ((), ())), preferred_element_type=jnp.float32
        )
        pieces = wide(ref[pl.ds(height, ROWS), pl.ds(0, height)])
        target_norms.append(pieces[0:1] + pieces[1:2] + pieces[2:3])
    norms = as_row(square_sums(train))
    count = len(outs).bit_length() - 1
    for d, out in enumerate(outs):
        turned = reverse_bits(d, count)
        number = jnp.where(core_ref[0] == 0, d, turned)
        picked = []
        for i in range(0, 2 * share, per):
            first = pl.multiple_of((i * len(outs)) + (number ^ feat) * per, per)
            picked.append(products[pl.ds(first, per), :])
        straight, crossed = (
            jnp.concatenate([x[:, i * share : (i + 1) * share] for x in target_norms], axis=1) for i in (d, turned)
        )
        here = jnp.concatenate(
            [jnp.where(core_ref[0] == 0, straight, crossed), jnp.zeros((1, rows - 2 * share), jnp.float32)], axis=1
        )
        sums = [norms, here]
        if d > 0:
            sums = [piece for row in sums for piece in pieces_of(row)]
        sums.append(jnp.zeros((out.shape[0] - 2 * share - len(sums), rows), jnp.float32))
        out[...] = jnp.concatenate([*picked, *sums], axis=0).astype(out.dtype)


def gram(feat_count, per, feat, core, mine, other, first, parts):
    total = 2 * (mine.shape[0] - ROWS)
    unused, last_rows, inner = parts[0].shape
    rows = first.shape[0] + last_rows

    def kernel(*refs):
        split = 5 + len(parts)
        gram_kernel(per, *refs[:5], refs[5:split], refs[split], refs[split + 1 : -1], refs[-1])

    last, *outs = call(
        kernel,
        [jax.ShapeDtypeStruct((last_rows, inner), jnp.bfloat16)]
        + [jax.ShapeDtypeStruct((total // feat_count + 8, rows), jnp.float32)]
        + [jax.ShapeDtypeStruct((total // feat_count + ROWS, rows), jnp.bfloat16)] * (feat_count - 1),
        [feat, core, mine, other, first, *parts],
        [SMEM, SMEM] + [VMEM] * (3 + len(parts)),
        "gram",
        scratch=[pltpu.VMEM((total, rows), jnp.float32)],
    )
    return last, outs


def inner_kernel(scale, table_ref, *refs):
    row = 0
    for ref in refs[:-1]:
        rows = ref.shape[0]
        refs[-1][pl.ds(row, rows), :] = inner_part(scale, table_ref[...], ref[...])
        row += rows


def inner_transform(scale, table, chunks):
    rows = sum(chunk.shape[0] for chunk in chunks)
    return call(
        functools.partial(inner_kernel, scale),
        jax.ShapeDtypeStruct((rows, chunks[0].shape[1]), jnp.bfloat16),
        [table, *chunks],
        [VMEM] * (1 + len(chunks)),
        "inner_transform",
        limit=16,
    )


def finish_kernel(mean_scale, per, ex_ref, projected_ref, *refs):
    parts, (features_ref, cosines_ref) = refs[:-2], refs[-2:]
    count = cosines_ref.shape[0]
    share = count // 2
    sums = parts[0][...]
    products, train_sums, target_sums = sums[:count], sums[count : count + 1], sums[count + 1 : count + 2]
    for part in parts[1:]:
        got = wide(part[...])
        products = products + got[:count]
        for i in range(count, count + 3):
            train_sums = train_sums + got[i : i + 1]
            target_sums = target_sums + got[i + 3 : i + 4]
    train_scale = lax.rsqrt(train_sums * mean_scale + EPS)
    target_scale = lax.rsqrt(target_sums[:, :count] * mean_scale + EPS)
    cosines = products * train_scale * as_column(target_scale) * mean_scale
    for i in range(count // per):
        group = ex_ref[0] ^ (i * 2 if i * per < share else i * 2 - count // per + 1)
        cosines_ref[pl.ds(pl.multiple_of(group * per, per), per), :] = cosines[i * per : (i + 1) * per]
    features_ref[...] = narrow(wide(projected_ref[...]) * as_column(train_scale))


def finish(mean_scale, per, ex, projected, parts):
    return call(
        functools.partial(finish_kernel, mean_scale, per),
        [
            jax.ShapeDtypeStruct(projected.shape, jnp.bfloat16),
            jax.ShapeDtypeStruct((parts[0].shape[0] - 8, projected.shape[0]), jnp.float32),
        ],
        [ex, projected, *parts],
        [SMEM] + [VMEM] * (1 + len(parts)),
        "finish",
    )


def swap(value, axis, distance):
    return lax.ppermute(value, axis, [(i, i ^ distance) for i in range(lax.axis_size(axis))])


def local(train_grads, target_grads, signs, block_order):
    train_grads, target_grads, signs, block_order = (
        pltpu.with_memory_space_constraint(value, pltpu.HBM)
        for value in (train_grads, target_grads, signs, block_order)
    )
    train_grads = pltpu.with_memory_space_constraint(train_grads, pltpu.VMEM)
    block_total, width = signs.shape
    feat_count = lax.axis_size("feat")
    groups = lax.axis_size("ex")
    feat = lax.axis_index("feat").astype(jnp.int32).reshape(1)
    ex = lax.axis_index("ex").astype(jnp.int32)
    train_rows, target_rows = train_grads.shape[0], target_grads.shape[0]
    per = target_rows // feat_count
    inner = width // feat_count
    mean_scale = 1.0 / (block_total * width * feat_count * SHRINK**2)
    scale = 1.0 / (math.sqrt(block_total * width) * SHRINK)
    table256 = inner_table(inner)
    bits = list(range(feat_count.bit_length() - 1))
    assert sum(CHUNKS) == train_rows

    core = (ex % 2).reshape(1)

    def turn(value, d):
        other = reverse_bits(d, len(bits))
        pairs = [
            (f * groups + e, (f ^ (d if e % 2 == 0 else other)) * groups + e)
            for f in range(feat_count)
            for e in range(groups)
        ]
        return lax.ppermute(value, ("feat", "ex"), pairs)

    target_parts, table = first_terms(feat_count, feat, core, block_order, signs, target_grads)
    own = pltpu.with_memory_space_constraint(target_parts[0], pltpu.VMEM)
    far = sorted(range(1, feat_count), key=lambda d: -d.bit_count())
    got = [own] + [turn(target_parts[d], d) for d in far]

    orders = [bits if i % 2 == 0 else bits[::-1] for i in range(len(CHUNKS))]
    firsts = [sum(CHUNKS[:i]) for i in range(len(CHUNKS))]

    def start(i, after):
        keep, send = terms(orders[i], core, table, train_grads, firsts[i], CHUNKS[i], after)
        return [keep, turn(send, 1 << orders[i][0])], send

    def proceed(order, parts, after):
        for bit in order[1:]:
            high = parts[-1].shape[0]
            send = after = middle(parts, high // 2, high, after)
            parts = [*parts, turn(send, 1 << bit)]
        return parts, after

    state = [None] * len(CHUNKS)
    state[0], mark = start(0, None)
    state[1], mark = start(1, mark)
    own = combine(got, mark)
    around = [own] + [swap(own, "ex", d) for d in range(2, groups, 2)]
    state[0], mark = proceed(orders[0], state[0], own)
    state[1], mark = proceed(orders[1], state[1], mark)
    mine = stack_targets(feat_count, per, feat, around, mark)
    other = swap(mine, "ex", 1)
    first = join(state[0])
    last, sums = gram(feat_count, per, feat, core, mine, other, first, state[1])
    sums = [sums[0]] + [turn(sums[d], d) for d in far]
    projected = inner_transform(scale, table256, [first, last])
    features, cosines = finish(mean_scale, per, ex.reshape(1), projected, sums)
    return features, cosines.reshape(groups, per, train_rows).transpose(2, 0, 1)


def solution(mesh):
    placed = (P("ex", "feat"), P("ex", "feat"), P(), P())
    return jax.shard_map(
        local,
        mesh=mesh,
        in_specs=placed,
        out_specs=(P("ex", "feat"), P("ex", None, "feat")),
        check_vma=False,
    )
```
